256 devices in a mesh: dp: 8 (over z), row: 32 (over y, x, core).
Axes of the slice: x: 4, y: 4, z: 8, core: 2. Of those that a mesh axis runs over, the one named last changes fastest.
Arguments:
- fields: bfloat16 [8, 16, 2048, 2048], P('dp', None, 'row'), may hold values from -6 to 6
- cotangent: bfloat16 [8, 16, 2048, 2048], P('dp', None, 'row'), may hold values from -6 to 6
- spectral: bfloat16 [2, 16, 16, 128, 128], P(None, None, None, 'row'), may hold values from -5 to 5
- local_weight: bfloat16 [16, 16], replicated, may hold values from -1.5 to 1.5
- bias: float32 [16], replicated, may hold values from -3 to 3
Outputs:
- field_grad: bfloat16 [8, 16, 2048, 2048], P('dp', None, 'row')
- spectral_grad: float32 [2, 16, 16, 128, 128], P(None, None, 'dp', 'row')
- local_grad: float32 [16, 16], replicated
- bias_grad: float32 [16], replicated
The draws below stay inside these ranges and needn't reach their ends.
All inputs are finite; a program needn't handle non-finite values.
Results may differ from the reference program's by a relative error of at most 0.028.
Values may be sent and summed in bfloat16 or wider, within the bound.
A program may use at most 128 MiB of HBM per device.

```python
import math
import jax
import jax.numpy as jnp
from jax import lax

C = 16
W = 2048
M = 128
H = 2048
NMAP = 8


def spiked(result, key, source, target, blocks, factor):
    owner, partner = [(jnp.arange(result.shape[position]) // (result.shape[position] // blocks)).reshape([-1 if axis == position else 1 for axis in range(result.ndim)]) for position in (source, target)]
    chosen = jax.random.permutation(key, blocks)[partner]
    strong = (owner == chosen) | (owner == (partner + blocks // 2) % blocks)
    return jnp.where(strong, factor * result, result)


def block_levels(key, shape, pieces, low, largest):
    def one(position, shards_of):
        steps = jax.random.uniform(jax.random.fold_in(jax.random.fold_in(key, 6), position), (shards_of,), jnp.float32, low / len(pieces), largest / len(pieces))
        return jnp.repeat(jnp.exp(steps), shape[position] // shards_of).reshape((-1,) + (1,) * (len(shape) - position - 1))

    gain = one(*pieces[0])
    for cut in pieces[1:]:
        gain = gain * one(*cut)
    return gain


def scatter_about(key, extent, scale, limit, pieces=(), kind=jnp.bfloat16):
    array = scale * jax.random.normal(key, extent, jnp.float32)
    if pieces:
        array = array * block_levels(key, extent, pieces, -0.22, 0.18)
    return jnp.clip(array, -limit, limit).astype(kind)


def gaussian_with(own_key, dims, scale, most, pieces, heavy, kind=jnp.bfloat16):
    drawn = scale * jax.random.normal(own_key, dims, jnp.float32)
    if pieces:
        drawn = drawn * block_levels(own_key, dims, pieces, -0.22, 0.18)
    return jnp.clip(spiked(drawn, jax.random.fold_in(own_key, 3), *heavy), -most, most).astype(kind)


def setup_inputs(seed: int = 0) -> dict:
    keys = jax.random.split(jax.random.key(seed), 6)
    fields = scatter_about(keys[0], (NMAP, C, H, W), 1.0, 6.0, ((0, 8), (2, 32)))
    cotangent = gaussian_with(keys[1], (NMAP, C, H, W), 1.0, 6.0, ((0, 8), (2, 32)), (0, 1, 8, 2.0))
    spectral = scatter_about(keys[2], (2, C, C, M, M), 1.0, 5.0, ((3, 32),))
    local_weight = scatter_about(keys[3], (C, C), C ** -0.5, 1.5)
    bias = scatter_about(keys[4], (C,), 0.5, 3.0, (), jnp.float32)
    return dict(fields=fields, cotangent=cotangent, spectral=spectral, local_weight=local_weight, bias=bias)


def phase_angle(freq, pos, count):
    turns = freq[:, None] % count * pos[None, :] % count
    return 2.0 * math.pi / count * turns.astype(jnp.float32)

def row_phases(first, length, height, modes):
    freq = jnp.arange(modes, dtype=jnp.int32) - modes // 2
    place = first + jnp.arange(length, dtype=jnp.int32)
    angle = phase_angle(freq, place, height)
    return jnp.stack([jnp.cos(angle), jnp.sin(angle)], axis=0).astype(jnp.bfloat16)

def column_forward(width, modes):
    angle = phase_angle(jnp.arange(modes, dtype=jnp.int32), jnp.arange(width, dtype=jnp.int32), width).T
    table = jnp.stack([jnp.cos(angle), -jnp.sin(angle)], axis=1)
    return table.reshape(width, 2 * modes).astype(jnp.bfloat16)

def column_inverse(width, modes, double):
    angle = phase_angle(jnp.arange(modes, dtype=jnp.int32), jnp.arange(width, dtype=jnp.int32), width)
    weight = jnp.where(jnp.arange(modes) == 0, 1.0, 2.0 if double else 1.0).astype(jnp.float32)[:, None]
    table = jnp.stack([weight * jnp.cos(angle), -weight * jnp.sin(angle)], axis=0)
    return table.reshape(2 * modes, width).astype(jnp.bfloat16)

def row_forward(phases, spectrum):
    parts = jnp.einsum('tah,chrb->tacrb', phases.astype(jnp.float32), spectrum.astype(jnp.float32))
    real = parts[0, :, :, 0] + parts[1, :, :, 1]
    imag = parts[0, :, :, 1] - parts[1, :, :, 0]
    return jnp.stack([real, imag], axis=2)

def row_inverse(phases, modes_in):
    parts = jnp.einsum('tah,aorb->tohrb', phases.astype(jnp.float32), modes_in.astype(jnp.float32))
    real = parts[0, :, :, 0] - parts[1, :, :, 1]
    imag = parts[0, :, :, 1] + parts[1, :, :, 0]
    return jnp.stack([real, imag], axis=2)

def product(left, right):
    return jnp.einsum('coab,acb->aob', left, right, precision=lax.Precision.HIGHEST)

def mix_modes(weights, spectrum):
    real = product(weights[0], spectrum[:, :, 0]) - product(weights[1], spectrum[:, :, 1])
    imag = product(weights[0], spectrum[:, :, 1]) + product(weights[1], spectrum[:, :, 0])
    return jnp.stack([real, imag], axis=2)

def outer(left, right):
    return jnp.einsum('aob,acb->coab', left, right, precision=lax.Precision.HIGHEST)

def back_product(weight, grad):
    return jnp.einsum('coab,aob->acb', weight, grad, precision=lax.Precision.HIGHEST)

def weight_terms(grad_modes, spectrum):
    real = outer(grad_modes[:, :, 0], spectrum[:, :, 0]) + outer(grad_modes[:, :, 1], spectrum[:, :, 1])
    imag = outer(grad_modes[:, :, 1], spectrum[:, :, 0]) - outer(grad_modes[:, :, 0], spectrum[:, :, 1])
    return jnp.stack([real, imag], axis=0)

def adjoint_modes(weights, grad_modes):
    real = back_product(weights[0], grad_modes[:, :, 0]) + back_product(weights[1], grad_modes[:, :, 1])
    imag = back_product(weights[0], grad_modes[:, :, 1]) - back_product(weights[1], grad_modes[:, :, 0])
    return jnp.stack([real, imag], axis=2)

def reference(fields, cotangent, spectral, local_weight, bias):
    norm_scale = 1.0 / math.sqrt(H * W)
    grad_scale = 1.0 / math.sqrt(NMAP * H * W)
    phases = row_phases(0, H, H, M)
    forward_cols = column_forward(W, M)
    inverse_double = column_inverse(W, M, True)
    inverse_single = column_inverse(W, M, False)
    doubling = jnp.where(jnp.arange(M) == 0, 1.0, 2.0).astype(jnp.float32)
    weights = spectral.astype(jnp.float32)
    local_float = local_weight.astype(jnp.float32)

    def one_map(pair):
        field, cot = pair
        coeffs = jnp.dot(field.reshape(C * H, W), forward_cols, preferred_element_type=jnp.float32)
        coeffs = coeffs.astype(jnp.bfloat16).reshape(C, H, 2, M)
        spectrum = norm_scale * row_forward(phases, coeffs)
        mixed = mix_modes(weights, spectrum).astype(jnp.bfloat16)
        back_rows = row_inverse(phases, mixed).astype(jnp.bfloat16)
        spec_out = norm_scale * jnp.dot(back_rows.reshape(C * H, 2 * M), inverse_double, preferred_element_type=jnp.float32).reshape(C, H, W)
        preact = spec_out + jnp.einsum('co,chw->ohw', local_float, field.astype(jnp.float32)) + bias[:, None, None]
        unused, pull = jax.vjp(jax.nn.gelu, preact)
        grad_pre = pull(cot.astype(jnp.float32))[0].astype(jnp.bfloat16)
        grad_coeffs = jnp.dot(grad_pre.reshape(C * H, W), forward_cols, preferred_element_type=jnp.float32)
        grad_coeffs = grad_coeffs.astype(jnp.bfloat16).reshape(C, H, 2, M)
        grad_modes = norm_scale * row_forward(phases, grad_coeffs) * doubling
        weight_term = weight_terms(grad_modes, spectrum)
        freq_grad = adjoint_modes(weights, grad_modes).astype(jnp.bfloat16)
        grad_rows = row_inverse(phases, freq_grad).astype(jnp.bfloat16)
        field_grad = norm_scale * jnp.dot(grad_rows.reshape(C * H, 2 * M), inverse_single, preferred_element_type=jnp.float32).reshape(C, H, W)
        field_grad = field_grad + jnp.einsum('co,ohw->chw', local_float, grad_pre.astype(jnp.float32))
        local_term = grad_scale * jnp.einsum('chw,ohw->co', field.astype(jnp.float32), grad_pre.astype(jnp.float32))
        bias_term = grad_scale * lax.optimization_barrier(jnp.sum(grad_pre.astype(jnp.float32), axis=(1, 2)))
        return (field_grad.astype(jnp.bfloat16), weight_term, local_term, bias_term)
    field_grad, weight_term, local_term, bias_term = lax.map(one_map, (fields, cotangent))
    return (field_grad, lax.optimization_barrier(jnp.sum(weight_term, axis=0)), lax.optimization_barrier(jnp.sum(local_term, axis=0)), lax.optimization_barrier(jnp.sum(bias_term, axis=0)))
```

```python
import functools
import math

import jax
import jax.numpy as jnp
import ml_dtypes
import numpy as np
from jax import lax
from jax.experimental import pallas as pl
from jax.experimental.pallas import tpu as pltpu
from jax.sharding import Mesh
from jax.sharding import PartitionSpec as P

ROW = ("row_0", "row_1", "row_2")
MESH = pl.DeviceIdType.MESH
F32 = jnp.float32
BF16 = jnp.bfloat16
SIDE = 4
CHIPS = SIDE * SIDE
GROUPS = 4
OFFSETS = (4, 0, 3, 5, 2, 6, 1, 7)
STEP = 512


def angles(freq, pos, count):
    turns = (freq[:, None] % count) * pos[None, :] % count
    return np.float32(2.0 * math.pi / count) * turns.astype(np.float32)


def column_tables(width, modes):
    angle = angles(np.arange(modes), np.arange(width), width)
    both = np.stack([np.cos(angle), -np.sin(angle)], axis=0).astype(ml_dtypes.bfloat16)
    inverse = both.reshape(2 * modes, width)
    return np.ascontiguousarray(inverse.T), inverse


def row_tables(height, modes, owners, scale):
    angle = angles(np.arange(modes) - modes // 2, np.arange(height), height)
    cos = np.cos(angle).astype(ml_dtypes.bfloat16).astype(np.float32) * scale
    sin = np.sin(angle).astype(ml_dtypes.bfloat16).astype(np.float32) * scale
    rows = height // owners
    each = modes // owners

    def split(table):
        table = table.reshape(CHIPS, 2, each, owners, rows)
        return table.transpose(3, 1, 0, 2, 4)

    cos, sin = split(cos), split(sin)
    forward = np.stack(
        [np.stack([cos, sin], axis=-2), np.stack([-sin, cos], axis=-2)], axis=3
    )
    half = forward.transpose(0, 5, 6, 1, 2, 3, 4)
    inverse = np.zeros((owners, 2) + half.shape[1:6] + (2, each), np.float32)
    for pair in range(2):
        inverse[:, pair, :, :, :, :, :, pair, :] = half
    forward = forward.reshape(owners, 2 * modes, 2 * rows)
    inverse = inverse.reshape(owners, 4 * rows, 4 * modes)
    return forward.astype(ml_dtypes.bfloat16), inverse.astype(ml_dtypes.bfloat16)


def dot(a, b):
    return jnp.dot(a, b, preferred_element_type=F32)


def wait_for(ref, sem):
    pltpu.make_async_copy(ref, ref, sem).wait()


def gelu_slope(x):
    k0 = math.sqrt(2.0 / math.pi)
    u = x * (k0 + (k0 * 0.044715) * (x * x))
    t = jnp.tanh(u)
    q = 1.5 * u - k0 * x
    return (1.0 + t) * (0.5 + q * (1.0 - t))


def spread_matrix(lw, transposed):
    i = lax.broadcasted_iota(jnp.int32, (256, 16), 0)
    j = lax.broadcasted_iota(jnp.int32, (256, 16), 1)
    pick = jnp.where(i // 16 == j, 1.0, 0.0).astype(BF16)
    if transposed:
        left = lax.dot_general(pick, lw, (((1,), (1,)), ((), ())), preferred_element_type=F32)
    else:
        left = dot(pick, lw)
    full = lax.dot_general(
        left.astype(BF16), pick, (((1,), (1,)), ((), ())), preferred_element_type=F32
    )
    i = lax.broadcasted_iota(jnp.int32, (256, 256), 0)
    j = lax.broadcasted_iota(jnp.int32, (256, 256), 1)
    return jnp.where(i % 16 == j % 16, full, 0.0).astype(BF16)


def exchange_kernel(
    fields, cot, spec, lw, bias, colf_h, coli_h, rowf_h, rowi_h,
    dy_o, lc_o, sg_o, sums_o,
    fbuf, cbuf, lbuf, gpbuf, lcbuf, wbf, wf, colf, coli, rowf, rowi,
    snd1, sib1, hb1, rcv1, snd2, sib2, hb2, rcv2, ga1, ga2,
    frd, fid, dfr, dfi, gbuf, ybuf, dybuf, bacc, lacc, dwsnd, dwrcv,
    pay, paysib, payrow, paydp,
    ld_f, ld, out_sem,
    ss1, rs1, ss2, rs2, ds1, dr1, ds2, dr2,
    as1, ar1, fs1, fr1, as2, ar2, fs2, fr2, dws, dwr, ps, pr,
):
    z = lax.axis_index("dp")
    y = lax.axis_index("row_0")
    x = lax.axis_index("row_1")
    core = lax.axis_index("row_2")
    other = 1 - core
    chip = y * SIDE + x
    row = chip * 2 + core

    barrier = pltpu.get_barrier_semaphore()

    def peer(k):
        ty = lax.rem(y + k // SIDE, SIDE)
        tx = lax.rem(x + k % SIDE, SIDE)
        return ty, tx

    for k in range(1, CHIPS):
        ty, tx = peer(k)
        pl.semaphore_signal(
            barrier, inc=1, device_id={"row_0": ty, "row_1": tx}, device_id_type=MESH
        )
    pl.semaphore_signal(barrier, inc=1, device_id={"row_2": other}, device_id_type=MESH)
    for k in range(1, 8):
        pl.semaphore_signal(
            barrier, inc=1, device_id={"dp": lax.rem(z + k, 8)}, device_id_type=MESH
        )

    def load(src, dst, sem):
        copy = pltpu.make_async_copy(src, dst, sem)
        copy.start()
        return copy

    l_colf = load(colf_h, colf, ld.at[0])
    l_f = [load(fields.at[pl.ds(0, 4)], fbuf.at[pl.ds(0, 4)], ld_f.at[0])]
    l_rowf = load(rowf_h.at[row], rowf, ld.at[1])
    for g in range(1, GROUPS):
        l_f.append(load(fields.at[pl.ds(4 * g, 4)], fbuf.at[pl.ds(4 * g, 4)], ld_f.at[g]))
    l_w = load(spec, wbf, ld.at[2])
    l_rowi = load(rowi_h.at[row], rowi, ld.at[3])
    l_coli = load(coli_h, coli, ld.at[4])
    l_cot = load(cot, cbuf, ld.at[5])

    def to_sibling(src, dst, ssem, rsem):
        pltpu.make_async_remote_copy(
            src_ref=src, dst_ref=dst, send_sem=ssem, recv_sem=rsem,
            device_id={"row_2": other}, device_id_type=MESH,
        ).start()

    def to_chips(src_of, dst, ssem, rsem):
        def body(k, carry):
            ty, tx = peer(k)
            pltpu.make_async_remote_copy(
                src_ref=src_of(ty * SIDE + tx), dst_ref=dst, send_sem=ssem, recv_sem=rsem,
                device_id={"row_0": ty, "row_1": tx}, device_id_type=MESH,
            ).start()
            return carry

        lax.fori_loop(1, CHIPS, body, 0)

    def row_transform(xb, snd, g):
        for j in range(2):
            cols = []
            for c in range(2):
                at = 128 * j + 64 * c
                cols.append(jnp.concatenate([xb[at : at + 64, :128], xb[at : at + 64, 128:]], axis=0))
            p = dot(rowf[...], jnp.concatenate(cols, axis=1))
            blk = jnp.concatenate(
                [p[:, :128].reshape(32, 8, 128), p[:, 128:].reshape(32, 8, 128)], axis=1
            ).astype(BF16)
            snd[g, :, :, 16 * j : 16 * j + 16, :] = blk.reshape(2, CHIPS, 16, 128)

    def start_sibling(snd, sib, ss, rs, g):
        to_sibling(snd.at[g, other], sib.at[g], ss.at[g], rs.at[g])

    def pass_on(snd, sib, hb, rcv, rs, ds, dr, g):
        wait_for(sib.at[g], rs.at[g])
        hb[g] = (snd[g, core].astype(F32) + sib[g].astype(F32)).astype(BF16)
        to_chips(lambda d: hb.at[g, d], rcv.at[g, chip], ds.at[g], dr.at[g])
        rcv[g, pl.ds(chip, 1)] = hb[g, pl.ds(chip, 1)]

    def arrived(rcv, dr, g):
        wait_for(rcv.at[g, pl.ds(0, CHIPS - 1)], dr.at[g])
        return jnp.sum(rcv[g].astype(F32), axis=0)

    def gather_start(ga, asem, arsem, g):
        to_chips(lambda d: ga.at[g, core, chip], ga.at[g, core, chip], asem.at[g], arsem.at[g])

    def gather_forward(ga, arsem, fs, fr, g):
        wait_for(ga.at[g, core, pl.ds(0, CHIPS - 1)], arsem.at[g])
        to_sibling(ga.at[g, core], ga.at[g, core], fs.at[g], fr.at[g])

    def gather_end(ga, fr, g):
        wait_for(ga.at[g, other], fr.at[g])

    def row_inverse(ga, g):
        parts = [ga[g, :, :, 16 * j : 16 * j + 16, :].reshape(512, 128) for j in range(2)]
        out = dot(rowi[...], jnp.concatenate(parts, axis=1)).astype(BF16)
        rows = []
        for j in range(2):
            for o in range(2):
                block = out[128 * o : 128 * o + 128, 128 * j : 128 * j + 128]
                rows.append(jnp.concatenate([block[:64], block[64:]], axis=1))
        return jnp.concatenate(rows, axis=0)

    l_colf.wait()
    for g in range(GROUPS):
        l_f[g].wait()
        xb = dot(fbuf[4 * g : 4 * g + 4].reshape(256, 2048), colf[...]).astype(BF16)
        if g == 0:
            l_rowf.wait()
        row_transform(xb, snd1, g)
        if g == 0:
            pl.semaphore_wait(barrier, CHIPS + 7)
        start_sibling(snd1, sib1, ss1, rs1, g)
        if g > 0:
            pass_on(snd1, sib1, hb1, rcv1, rs1, ds1, dr1, g - 1)

    i = lax.broadcasted_iota(jnp.int32, (256, 16), 0)
    j = lax.broadcasted_iota(jnp.int32, (256, 16), 1)
    bias_col = jnp.sum(jnp.where(i // 16 == j, bias[...], 0.0), axis=1, keepdims=True)
    mix_fwd = spread_matrix(lw[...], True)

    def local_block(block):
        at = pl.ds(pl.multiple_of(block * 16, 16), 16)
        for w in range(0, 2048, STEP):
            part = dot(mix_fwd, fbuf[:, at, w : w + STEP].reshape(256, STEP)) + bias_col
            lbuf[:, at, w : w + STEP] = part.reshape(16, 16, STEP)

    local_block(0)
    pass_on(snd1, sib1, hb1, rcv1, rs1, ds1, dr1, GROUPS - 1)
    local_block(1)
    l_w.wait()

    def widen(c, carry):
        at = pl.ds(pl.multiple_of(c * 64, 64), 64)
        for part in range(2):
            wf[part, c] = wbf[part, at, :].astype(F32).reshape(8, 8, 128)
        return carry

    lax.fori_loop(0, 16, widen, 0)

    for g in range(GROUPS):
        total = arrived(rcv1, dr1, g)
        for c in range(4):
            real = total[8 * c : 8 * c + 4]
            imag = total[8 * c + 4 : 8 * c + 8]
            frd[4 * g + c] = jnp.concatenate([real, real], axis=0)
            fid[4 * g + c] = jnp.concatenate([imag, imag], axis=0)

    lane = lax.broadcasted_iota(jnp.int32, (8, 128), 1)
    double = jnp.where(lane == 0, 1.0, 2.0).astype(F32)

    def mix(c, carry):
        real, imag = carry
        wr, wi = wf[0, c], wf[1, c]
        fr, fi = frd[c][None], fid[c][None]
        return real + wr * fr - wi * fi, imag + wr * fi + wi * fr

    zero = jnp.zeros((8, 8, 128), F32)
    real, imag = lax.fori_loop(0, 16, mix, (zero, zero))
    gbuf[...] = (jnp.concatenate([real, imag], axis=1) * jnp.concatenate([double, double], axis=0)).astype(BF16)

    def pair_at(p):
        return lax.rem(z + OFFSETS[p], 8)

    for g in range(GROUPS):
        for j in range(2):
            ga1[g, core, chip, 16 * j : 16 * j + 16, :] = gbuf[pair_at(2 * g + j)]
        gather_start(ga1, as1, ar1, g)
    local_block(2)
    local_block(3)
    l_cot.wait()
    l_rowi.wait()
    l_coli.wait()
    gather_forward(ga1, ar1, fs1, fr1, 0)
    dfr[...] = jnp.zeros_like(dfr)
    dfi[...] = jnp.zeros_like(dfi)

    def gradient_arrived(g):
        total = arrived(rcv2, dr2, g)
        for j in range(2):
            q = pair_at(2 * g + j)
            a, b = total[16 * j : 16 * j + 8], total[16 * j + 8 : 16 * j + 16]
            gr = jnp.concatenate([a[:4], b[:4]], axis=0) * double
            gi = jnp.concatenate([a[4:], b[4:]], axis=0) * double
            slot = 2 * g + j
            wr = wf[0, :, pl.ds(q, 1)].reshape(16, 8, 128)
            wi = wf[1, :, pl.ds(q, 1)].reshape(16, 8, 128)
            fr, fi = frd[...], fid[...]
            dfr[...] += wr * gr[None] + wi * gi[None]
            dfi[...] += wr * gi[None] - wi * gr[None]
            term = jnp.concatenate(
                [
                    (gr[None] * fr + gi[None] * fi).reshape(128, 128),
                    (gi[None] * fr - gr[None] * fi).reshape(128, 128),
                ],
                axis=0,
            ).astype(BF16)
            if OFFSETS[slot] == 0:
                dwrcv[pl.ds(z, 1)] = term[None]
            else:
                dwsnd[slot] = term
                pltpu.make_async_remote_copy(
                    src_ref=dwsnd.at[slot], dst_ref=dwrcv.at[z], send_sem=dws.at[slot],
                    recv_sem=dwr, device_id={"dp": q}, device_id_type=MESH,
                ).start()

    for g in range(GROUPS):
        gather_end(ga1, fr1, g)
        ybuf[...] = row_inverse(ga1, g)
        pairs = [pair_at(2 * g), pair_at(2 * g + 1)]

        def chunk(w, acc):
            at = pl.ds(pl.multiple_of(w * STEP, STEP), STEP)
            out = dot(ybuf[...], coli[:, at])
            grads = []
            for j in range(2):
                o = pl.ds(2 * pairs[j], 2)
                pre = out[128 * j : 128 * j + 128] + lbuf[o, :, at].reshape(128, STEP)
                grad = cbuf[o, :, at].reshape(128, STEP).astype(F32) * gelu_slope(pre)
                grad = grad.astype(BF16)
                gpbuf[o, :, at] = grad.reshape(2, 64, STEP)
                grads.append(grad)
            return acc + dot(jnp.concatenate(grads, axis=0), colf[at, :])

        acc = lax.fori_loop(0, 2, chunk, jnp.zeros((256, 256), F32))
        if g > 0:
            pass_on(snd2, sib2, hb2, rcv2, rs2, ds2, dr2, g - 1)
        if g + 1 < GROUPS:
            gather_forward(ga1, ar1, fs1, fr1, g + 1)
        acc = lax.fori_loop(2, 4, chunk, acc)
        for j in range(2):
            for o in range(2):
                at = 128 * j + 64 * o
                bacc[2 * pairs[j] + o] = jnp.sum(acc[at : at + 64, :128].reshape(8, 8, 128), axis=0)
        row_transform(acc.astype(BF16), snd2, g)
        start_sibling(snd2, sib2, ss2, rs2, g)
        if g > 1:
            gradient_arrived(g - 2)

    nt = (((1,), (1,)), ((), ()))

    def outer_block(block):
        at = pl.ds(block * 16, 16)
        return lax.dot_general(
            fbuf[:, at, :].reshape(256, 2048), gpbuf[:, at, :].reshape(256, 2048), nt,
            preferred_element_type=F32,
        )

    mix_bwd = spread_matrix(lw[...], False)
    lc_copies = []

    def back_block(block):
        at = pl.ds(block * 16, 16)
        for w in range(0, 2048, STEP):
            part = dot(mix_bwd, gpbuf[:, at, w : w + STEP].reshape(256, STEP))
            lcbuf[:, at, w : w + STEP] = part.astype(BF16).reshape(16, 16, STEP)
        copy = pltpu.make_async_copy(lcbuf.at[:, at, :], lc_o.at[:, at, :], out_sem.at[block])
        copy.start()
        lc_copies.append(copy)

    lacc[...] = outer_block(0)
    pass_on(snd2, sib2, hb2, rcv2, rs2, ds2, dr2, GROUPS - 1)
    lacc[...] += outer_block(1)
    gradient_arrived(GROUPS - 2)
    lacc[...] += outer_block(2)
    lacc[...] += outer_block(3)

    i = lax.broadcasted_iota(jnp.int32, (256, 256), 0)
    j = lax.broadcasted_iota(jnp.int32, (256, 256), 1)
    kept = jnp.where(i % 16 == j % 16, lacc[...], 0.0)
    kept = jnp.sum(kept.reshape(16, 16, 256), axis=1)
    i = lax.broadcasted_iota(jnp.int32, (256, 128), 0)
    j = lax.broadcasted_iota(jnp.int32, (256, 128), 1)
    pick = jnp.where(i // 16 == j, 1.0, 0.0).astype(F32)
    local = jnp.dot(kept, pick, preferred_element_type=F32, precision=lax.Precision.HIGHEST)
    first = jnp.sum(jnp.sum(bacc[...], axis=1)[:, :1], axis=1, keepdims=True)
    lane16 = lax.broadcasted_iota(jnp.int32, (16, 128), 1)
    pay[0] = jnp.where(lane16 == 16, first, local)
    to_sibling(pay.at[0], paysib, ps.at[0], pr.at[0])

    gradient_arrived(GROUPS - 1)

    for g in range(GROUPS):
        for j in range(2):
            c = 4 * g + 2 * j
            parts = []
            for ref in (dfr, dfi):
                for k in range(2):
                    both = ref[c + k]
                    parts.append(both[:4] + both[4:])
            ga2[g, core, chip, 16 * j : 16 * j + 16, :] = jnp.concatenate(parts, axis=0).astype(BF16)
        gather_start(ga2, as2, ar2, g)

    back_block(0)
    wait_for(paysib, pr.at[0])
    pay[1] = pay[0] + paysib[...]
    to_chips(lambda d: pay.at[1], payrow.at[chip], ps.at[1], pr.at[1])
    payrow[pl.ds(chip, 1)] = pay[pl.ds(1, 1)]
    back_block(1)
    back_block(2)
    back_block(3)
    wait_for(payrow.at[pl.ds(0, CHIPS - 1)], pr.at[1])
    pay[2] = jnp.sum(payrow[...], axis=0)
    for k in range(1, 8):
        pltpu.make_async_remote_copy(
            src_ref=pay.at[2], dst_ref=paydp.at[z], send_sem=ps.at[2], recv_sem=pr.at[2],
            device_id={"dp": lax.rem(z + k, 8)}, device_id_type=MESH,
        ).start()
    paydp[pl.ds(z, 1)] = pay[pl.ds(2, 1)]

    dy_copies = []
    gather_forward(ga2, ar2, fs2, fr2, 0)
    for g in range(GROUPS):
        if g + 1 < GROUPS:
            gather_forward(ga2, ar2, fs2, fr2, g + 1)
        gather_end(ga2, fr2, g)
        dybuf[4 * g : 4 * g + 4] = row_inverse(ga2, g).reshape(4, 64, 256)
        copy = pltpu.make_async_copy(
            dybuf.at[pl.ds(4 * g, 4)], dy_o.at[pl.ds(4 * g, 4)], out_sem.at[4 + g]
        )
        copy.start()
        dy_copies.append(copy)

    wait_for(dwrcv.at[pl.ds(0, 7)], dwr)
    total = dwrcv[0].astype(F32)
    for k in range(1, 8):
        total = total + dwrcv[k].astype(F32)
    sg_o[...] = total.reshape(32, 8, 128)

    wait_for(paydp.at[pl.ds(0, 7)], pr.at[2])
    scale = 1.0 / math.sqrt(8 * 2048 * 2048)
    sums_o[...] = scale * jnp.sum(paydp[...], axis=0)

    for g in range(GROUPS):
        wait_for(snd1.at[g, 0], ss1.at[g])
        wait_for(hb1.at[g, pl.ds(0, CHIPS - 1)], ds1.at[g])
        wait_for(snd2.at[g, 0], ss2.at[g])
        wait_for(hb2.at[g, pl.ds(0, CHIPS - 1)], ds2.at[g])
        wait_for(ga1.at[g, core, pl.ds(0, CHIPS - 1)], as1.at[g])
        wait_for(ga1.at[g, core], fs1.at[g])
        wait_for(ga2.at[g, core, pl.ds(0, CHIPS - 1)], as2.at[g])
        wait_for(ga2.at[g, core], fs2.at[g])
    for slot in range(8):
        if OFFSETS[slot] != 0:
            wait_for(dwsnd.at[slot], dws.at[slot])
    wait_for(pay.at[0], ps.at[0])
    wait_for(payrow.at[pl.ds(0, CHIPS - 1)], ps.at[1])
    wait_for(paydp.at[pl.ds(0, 7)], ps.at[2])
    for copy in lc_copies + dy_copies:
        copy.wait()


def combine_kernel(dy, lc, coli, out):
    chans = dy.shape[0]
    spectral = dot(dy[...].reshape(chans * 64, 256), coli[...])
    out[...] = (spectral + lc[...].reshape(chans * 64, 2048).astype(F32)).astype(BF16).reshape(out.shape)


def on_device(fields, cotangent, spectral, local_weight, bias):
    chans, rows, width = fields.shape[1:]
    modes = spectral.shape[4]
    height = rows * 2 * CHIPS
    scale = 1.0 / math.sqrt(height * width)
    colf, coli = column_tables(width, modes)
    rowf, rowi = row_tables(height, modes, 2 * CHIPS, scale)
    colf, coli, rowf, rowi = (jnp.asarray(t) for t in (colf, coli, rowf, rowi))
    anywhere = pl.BlockSpec(memory_space=pl.ANY)
    vmem = pl.BlockSpec(memory_space=pltpu.VMEM)
    dma = pltpu.SemaphoreType.DMA
    big = (16, 64, 2048)
    reduce_bufs = [
        pltpu.VMEM((GROUPS, 2, CHIPS, 32, 128), BF16),
        pltpu.VMEM((GROUPS, CHIPS, 32, 128), BF16),
        pltpu.VMEM((GROUPS, CHIPS, 32, 128), BF16),
        pltpu.VMEM((GROUPS, CHIPS, 32, 128), BF16),
    ]
    gather_buf = pltpu.VMEM((GROUPS, 2, CHIPS, 32, 128), BF16)
    tile16 = pltpu.VMEM((16, 8, 128), F32)
    scratch = [
        pltpu.VMEM(big, BF16),
        pltpu.VMEM(big, BF16),
        pltpu.VMEM(big, F32),
        pltpu.VMEM(big, BF16),
        pltpu.VMEM(big, BF16),
        pltpu.VMEM((2, 1024, 128), BF16),
        pltpu.VMEM((2, 16, 8, 8, 128), F32),
        pltpu.VMEM(colf.shape, BF16),
        pltpu.VMEM(coli.shape, BF16),
        pltpu.VMEM(rowf.shape[1:], BF16),
        pltpu.VMEM(rowi.shape[1:], BF16),
        *reduce_bufs,
        *reduce_bufs,
        gather_buf,
        gather_buf,
        tile16,
        tile16,
        tile16,
        tile16,
        pltpu.VMEM((8, 16, 128), BF16),
        pltpu.VMEM((256, 256), BF16),
        pltpu.VMEM((16, 64, 256), BF16),
        tile16,
        pltpu.VMEM((256, 256), F32),
        pltpu.VMEM((8, 256, 128), BF16),
        pltpu.VMEM((8, 256, 128), BF16),
        pltpu.VMEM((3, 16, 128), F32),
        pltpu.VMEM((16, 128), F32),
        pltpu.VMEM((CHIPS, 16, 128), F32),
        pltpu.VMEM((8, 16, 128), F32),
        dma((GROUPS,)),
        dma((6,)),
        dma((8,)),
        *[dma((GROUPS,)) for _ in range(16)],
        dma((8,)),
        dma(()),
        dma((3,)),
        dma((3,)),
    ]
    dy, lc, sg, sums = pl.pallas_call(
        exchange_kernel,
        out_shape=(
            jax.ShapeDtypeStruct((16, 64, 256), BF16),
            jax.ShapeDtypeStruct(big, BF16),
            jax.ShapeDtypeStruct((32, 8, 128), F32),
            jax.ShapeDtypeStruct((16, 128), F32),
        ),
        in_specs=[anywhere, anywhere, anywhere, vmem, vmem, anywhere, anywhere, anywhere, anywhere],
        out_specs=(anywhere, anywhere, vmem, vmem),
        scratch_shapes=scratch,
        compiler_params=pltpu.CompilerParams(
            collective_id=0, has_side_effects=True, vmem_limit_bytes=58 * 2**20
        ),
        cost_estimate=pl.CostEstimate(flops=8 * 10**9, bytes_accessed=16 * 2**20, transcendentals=2**21),
        name="layer_exchange",
    )(
        fields[0], cotangent[0], spectral.reshape(2, 1024, 128), local_weight, bias[None, :],
        colf, coli, rowf, rowi,
    )
    step = 2
    grad = pl.pallas_call(
        combine_kernel,
        grid=(chans // step,),
        out_shape=jax.ShapeDtypeStruct((1,) + big, BF16),
        in_specs=[
            pl.BlockSpec((step, 64, 256), lambda i: (i, 0, 0)),
            pl.BlockSpec((step, 64, 2048), lambda i: (i, 0, 0)),
            pl.BlockSpec((256, 2048), lambda i: (0, 0)),
        ],
        out_specs=pl.BlockSpec((1, step, 64, 2048), lambda i: (0, i, 0, 0)),
        compiler_params=pltpu.CompilerParams(vmem_limit_bytes=32 * 2**20),
        cost_estimate=pl.CostEstimate(flops=10**9, bytes_accessed=9 * 2**20, transcendentals=0),
        name="map_gradient",
    )(dy, lc, coli)
    return grad, sg.reshape(2, 16, 2, 4, 128), sums[:, :16], sums[:, 16]


def solution(mesh):
    finer = Mesh(mesh.devices.reshape(mesh.shape["dp"], 4, 4, 2), ("dp", "row_0", "row_1", "row_2"))
    placed = (
        P("dp", None, ROW, None),
        P("dp", None, ROW, None),
        P(None, None, None, ROW, None),
        P(),
        P(),
    )
    return jax.shard_map(
        on_device,
        mesh=finer,
        in_specs=placed,
        out_specs=(P("dp", None, ROW, None), P(None, None, "dp", ROW, None), P(), P()),
        check_vma=False,
    )
```

```python
import functools
import math

import jax
import jax.numpy as jnp
import ml_dtypes
import numpy as np
from jax import lax
from jax.experimental import pallas as pl
from jax.experimental.pallas import tpu as pltpu
from jax.sharding import Mesh
from jax.sharding import PartitionSpec as P

ROW = ("row_0", "row_1", "row_2")
MESH = pl.DeviceIdType.MESH
F32 = jnp.float32
BF16 = jnp.bfloat16
SIDE = 4
CHIPS = SIDE * SIDE
GROUPS = 4
OFFSETS = (4, 0, 3, 5, 2, 6, 1, 7)
STEP = 512
PEERS = sorted(
    ((dy, dx) for dy in range(SIDE) for dx in range(SIDE) if dy or dx),
    key=lambda p: -(min(p[0], SIDE - p[0]) + min(p[1], SIDE - p[1])),
)


def angles(freq, pos, count):
    turns = (freq[:, None] % count) * pos[None, :] % count
    return np.float32(2.0 * math.pi / count) * turns.astype(np.float32)


def column_tables(width, modes):
    angle = angles(np.arange(modes), np.arange(width), width)
    both = np.stack([np.cos(angle), -np.sin(angle)], axis=0).astype(ml_dtypes.bfloat16)
    inverse = both.reshape(2 * modes, width)
    return np.ascontiguousarray(inverse.T), inverse


def row_tables(height, modes, owners, scale):
    angle = angles(np.arange(modes) - modes // 2, np.arange(height), height)
    cos = np.cos(angle).astype(ml_dtypes.bfloat16).astype(np.float32) * scale
    sin = np.sin(angle).astype(ml_dtypes.bfloat16).astype(np.float32) * scale
    rows = height // owners
    each = modes // owners

    def split(table):
        table = table.reshape(CHIPS, 2, each, owners, rows)
        return table.transpose(3, 1, 0, 2, 4)

    cos, sin = split(cos), split(sin)
    forward = np.stack(
        [np.stack([cos, sin], axis=-2), np.stack([-sin, cos], axis=-2)], axis=3
    )
    half = forward.transpose(0, 5, 6, 1, 2, 3, 4)
    inverse = np.zeros((owners, 2) + half.shape[1:6] + (2, each), np.float32)
    for pair in range(2):
        inverse[:, pair, :, :, :, :, :, pair, :] = half
    forward = forward.reshape(owners, 2 * modes, 2 * rows)
    inverse = inverse.reshape(owners, 4 * rows, 4 * modes)
    return forward.astype(ml_dtypes.bfloat16), inverse.astype(ml_dtypes.bfloat16)


def dot(a, b):
    return jnp.dot(a, b, preferred_element_type=F32)


def wait_for(ref, sem):
    pltpu.make_async_copy(ref, ref, sem).wait()


def gelu_slope(x):
    k0 = math.sqrt(2.0 / math.pi)
    one = BF16
    x = x.astype(BF16)
    a = one(k0 * 0.044715) * (x * x)
    t = jnp.tanh(x * (a + one(k0)))
    q = x * (one(1.5) * a + one(0.5 * k0))
    return (one(1.0) + t) * (one(0.5) + q * (one(1.0) - t))


def spread_matrix(lw, transposed):
    i = lax.broadcasted_iota(jnp.int32, (256, 16), 0)
    j = lax.broadcasted_iota(jnp.int32, (256, 16), 1)
    pick = jnp.where(i // 16 == j, 1.0, 0.0).astype(BF16)
    if transposed:
        left = lax.dot_general(pick, lw, (((1,), (1,)), ((), ())), preferred_element_type=F32)
    else:
        left = dot(pick, lw)
    full = lax.dot_general(
        left.astype(BF16), pick, (((1,), (1,)), ((), ())), preferred_element_type=F32
    )
    i = lax.broadcasted_iota(jnp.int32, (256, 256), 0)
    j = lax.broadcasted_iota(jnp.int32, (256, 256), 1)
    return jnp.where(i % 16 == j % 16, full, 0.0).astype(BF16)


def exchange_kernel(
    fields, cot, spec, lw_h, bias_h, colf_h, coli_h, rowf_h, rowi_h,
    fg_o, sg_o, sums_o,
    lw, bias, fbuf, cbuf, lbuf, gpbuf, wbf, wf, colf, coli, rowf, rowi,
    snd1, sib1, hb1, rcv1, snd2, sib2, hb2, rcv2, ga1, ga2,
    frd, fid, dfr, dfi, gbuf, ybuf, bacc, lacc, dwsnd, dwrcv,
    pay, paysib, payrow, paydp,
    ld_f, ld,
    ss1, rs1, ss2, rs2, ds1, dr1, ds2, dr2,
    as1, ar1, fs1, fr1, as2, ar2, fs2, fr2, dws, dwr, ps, pr,
):
    z = lax.axis_index("dp")
    y = lax.axis_index("row_0")
    x = lax.axis_index("row_1")
    core = lax.axis_index("row_2")
    other = 1 - core
    chip = y * SIDE + x
    row = chip * 2 + core

    barrier = pltpu.get_barrier_semaphore()

    rows_y = [lax.rem(y + d, SIDE) for d in range(SIDE)]
    rows_x = [lax.rem(x + d, SIDE) for d in range(SIDE)]
    peers = [(rows_y[dy], rows_x[dx]) for dy, dx in PEERS]

    for ty, tx in peers:
        pl.semaphore_signal(
            barrier, inc=1, device_id={"row_0": ty, "row_1": tx}, device_id_type=MESH
        )
    pl.semaphore_signal(barrier, inc=1, device_id={"row_2": other}, device_id_type=MESH)
    for k in range(1, 8):
        pl.semaphore_signal(
            barrier, inc=1, device_id={"dp": lax.rem(z + k, 8)}, device_id_type=MESH
        )

    def load(src, dst, sem):
        copy = pltpu.make_async_copy(src, dst, sem)
        copy.start()
        return copy

    l_colf = load(colf_h, colf, ld.at[0])
    l_f = [load(fields.at[pl.ds(0, 4)], fbuf.at[pl.ds(0, 4)], ld_f.at[0])]
    l_rowf = load(rowf_h.at[row], rowf, ld.at[1])
    for g in range(1, GROUPS):
        l_f.append(load(fields.at[pl.ds(4 * g, 4)], fbuf.at[pl.ds(4 * g, 4)], ld_f.at[g]))
    l_w = load(spec, wbf, ld.at[2])
    l_lw = load(lw_h, lw, ld.at[6])
    l_bias = load(bias_h, bias, ld.at[7])
    l_rowi = load(rowi_h.at[row], rowi, ld.at[3])
    l_coli = load(coli_h, coli, ld.at[4])
    l_cot = load(cot, cbuf, ld.at[5])

    def to_sibling(src, dst, ssem, rsem):
        pltpu.make_async_remote_copy(
            src_ref=src, dst_ref=dst, send_sem=ssem, recv_sem=rsem,
            device_id={"row_2": other}, device_id_type=MESH,
        ).start()

    def to_chips(src_of, dst, ssem, rsem):
        for ty, tx in peers:
            pltpu.make_async_remote_copy(
                src_ref=src_of(ty * SIDE + tx), dst_ref=dst, send_sem=ssem, recv_sem=rsem,
                device_id={"row_0": ty, "row_1": tx}, device_id_type=MESH,
            ).start()

    def row_transform(xb, snd, g):
        for j in range(2):
            cols = []
            for c in range(2):
                at = 128 * j + 64 * c
                cols.append(jnp.concatenate([xb[at : at + 64, :128], xb[at : at + 64, 128:]], axis=0))
            p = dot(rowf[...], jnp.concatenate(cols, axis=1))
            blk = jnp.concatenate(
                [p[:, :128].reshape(32, 8, 128), p[:, 128:].reshape(32, 8, 128)], axis=1
            ).astype(BF16)
            snd[g, :, :, 16 * j : 16 * j + 16, :] = blk.reshape(2, CHIPS, 16, 128)

    def start_sibling(snd, sib, ss, rs, g):
        to_sibling(snd.at[g, other], sib.at[g], ss.at[g], rs.at[g])

    def pass_on(snd, sib, hb, rcv, rs, ds, dr, g):
        wait_for(sib.at[g], rs.at[g])
        hb[g] = (snd[g, core].astype(F32) + sib[g].astype(F32)).astype(BF16)
        to_chips(lambda d: hb.at[g, d], rcv.at[g, chip], ds.at[g], dr.at[g])
        rcv[g, pl.ds(chip, 1)] = hb[g, pl.ds(chip, 1)]

    def arrived(rcv, dr, g):
        wait_for(rcv.at[g, pl.ds(0, CHIPS - 1)], dr.at[g])
        return jnp.sum(rcv[g].astype(F32), axis=0)

    def gather_start(ga, asem, arsem, g):
        to_chips(lambda d: ga.at[g, core, chip], ga.at[g, core, chip], asem.at[g], arsem.at[g])

    def gather_forward(ga, arsem, fs, fr, g):
        wait_for(ga.at[g, core, pl.ds(0, CHIPS - 1)], arsem.at[g])
        to_sibling(ga.at[g, core], ga.at[g, core], fs.at[g], fr.at[g])

    def gather_end(ga, fr, g):
        wait_for(ga.at[g, other], fr.at[g])

    def row_inverse(ga, g):
        parts = [ga[g, :, :, 16 * j : 16 * j + 16, :].reshape(512, 128) for j in range(2)]
        out = dot(rowi[...], jnp.concatenate(parts, axis=1)).astype(BF16)
        rows = []
        for j in range(2):
            for o in range(2):
                block = out[128 * o : 128 * o + 128, 128 * j : 128 * j + 128]
                rows.append(jnp.concatenate([block[:64], block[64:]], axis=1))
        return jnp.concatenate(rows, axis=0)

    l_colf.wait()
    for g in range(GROUPS):
        l_f[g].wait()
        xb = dot(fbuf[4 * g : 4 * g + 4].reshape(256, 2048), colf[...]).astype(BF16)
        if g == 0:
            l_rowf.wait()
        row_transform(xb, snd1, g)
        if g == GROUPS - 2:
            pl.semaphore_wait(barrier, CHIPS + 7)
            for early in range(GROUPS - 1):
                start_sibling(snd1, sib1, ss1, rs1, early)
    start_sibling(snd1, sib1, ss1, rs1, GROUPS - 1)
    for g in range(GROUPS):
        pass_on(snd1, sib1, hb1, rcv1, rs1, ds1, dr1, g)

    l_lw.wait()
    l_bias.wait()
    i = lax.broadcasted_iota(jnp.int32, (256, 16), 0)
    j = lax.broadcasted_iota(jnp.int32, (256, 16), 1)
    bias_col = jnp.sum(jnp.where(i // 16 == j, bias[...], 0.0), axis=1, keepdims=True)
    mix_fwd = spread_matrix(lw[...], True)

    def local_block(block):
        at = pl.ds(pl.multiple_of(block * 16, 16), 16)
        for w in range(0, 2048, STEP):
            part = dot(mix_fwd, fbuf[:, at, w : w + STEP].reshape(256, STEP)) + bias_col
            lbuf[:, at, w : w + STEP] = part.reshape(16, 16, STEP)

    local_block(0)
    local_block(1)
    l_w.wait()

    def widen(c, carry):
        at = pl.ds(pl.multiple_of(c * 64, 64), 64)
        for part in range(2):
            wf[part, c] = wbf[part, at, :].astype(F32).reshape(8, 8, 128)
        return carry

    lax.fori_loop(0, 16, widen, 0)

    for g in range(GROUPS):
        total = arrived(rcv1, dr1, g)
        for c in range(4):
            real = total[8 * c : 8 * c + 4]
            imag = total[8 * c + 4 : 8 * c + 8]
            frd[4 * g + c] = jnp.concatenate([real, real], axis=0)
            fid[4 * g + c] = jnp.concatenate([imag, imag], axis=0)

    lane = lax.broadcasted_iota(jnp.int32, (8, 128), 1)
    double = jnp.where(lane == 0, 1.0, 2.0).astype(F32)

    def mix(c, carry):
        real, imag = carry
        wr, wi = wf[0, c], wf[1, c]
        fr, fi = frd[c][None], fid[c][None]
        return real + wr * fr - wi * fi, imag + wr * fi + wi * fr

    zero = jnp.zeros((8, 8, 128), F32)
    real, imag = lax.fori_loop(0, 16, mix, (zero, zero))
    gbuf[...] = (jnp.concatenate([real, imag], axis=1) * jnp.concatenate([double, double], axis=0)).astype(BF16)

    def pair_at(p):
        return lax.rem(z + OFFSETS[p], 8)

    for g in range(GROUPS):
        for j in range(2):
            ga1[g, core, chip, 16 * j : 16 * j + 16, :] = gbuf[pair_at(2 * g + j)]
        gather_start(ga1, as1, ar1, g)
    local_block(2)
    local_block(3)
    l_cot.wait()
    l_rowi.wait()
    l_coli.wait()
    gather_forward(ga1, ar1, fs1, fr1, 0)
    dfr[...] = jnp.zeros_like(dfr)
    dfi[...] = jnp.zeros_like(dfi)

    def gradient_arrived(g):
        total = arrived(rcv2, dr2, g)
        for j in range(2):
            q = pair_at(2 * g + j)
            a, b = total[16 * j : 16 * j + 8], total[16 * j + 8 : 16 * j + 16]
            gr = jnp.concatenate([a[:4], b[:4]], axis=0) * double
            gi = jnp.concatenate([a[4:], b[4:]], axis=0) * double
            slot = 2 * g + j
            wr = wf[0, :, pl.ds(q, 1)].reshape(16, 8, 128)
            wi = wf[1, :, pl.ds(q, 1)].reshape(16, 8, 128)
            fr, fi = frd[...], fid[...]
            dfr[...] += wr * gr[None] + wi * gi[None]
            dfi[...] += wr * gi[None] - wi * gr[None]
            term = jnp.concatenate(
                [
                    (gr[None] * fr + gi[None] * fi).reshape(128, 128),
                    (gi[None] * fr - gr[None] * fi).reshape(128, 128),
                ],
                axis=0,
            ).astype(BF16)
            if OFFSETS[slot] == 0:
                dwrcv[pl.ds(z, 1)] = term[None]
            else:
                dwsnd[slot] = term
                pltpu.make_async_remote_copy(
                    src_ref=dwsnd.at[slot], dst_ref=dwrcv.at[z], send_sem=dws.at[slot],
                    recv_sem=dwr, device_id={"dp": q}, device_id_type=MESH,
                ).start()

    for g in range(GROUPS):
        gather_end(ga1, fr1, g)
        ybuf[...] = row_inverse(ga1, g)
        pairs = [pair_at(2 * g), pair_at(2 * g + 1)]

        def chunk(w, acc):
            at = pl.ds(w * STEP, STEP)
            out = dot(ybuf[...], coli[:, at])
            grads = []
            for j in range(2):
                o = pl.ds(2 * pairs[j], 2)
                pre = out[128 * j : 128 * j + 128] + lbuf[o, :, at].reshape(128, STEP)
                grad = cbuf[o, :, at].reshape(128, STEP) * gelu_slope(pre)
                gpbuf[o, :, at] = grad.reshape(2, 64, STEP)
                grads.append(grad)
            return acc + dot(jnp.concatenate(grads, axis=0), colf[at, :])

        acc = chunk(1, chunk(0, jnp.zeros((256, 256), F32)))
        if g > 0:
            pass_on(snd2, sib2, hb2, rcv2, rs2, ds2, dr2, g - 1)
        if g + 1 < GROUPS:
            gather_forward(ga1, ar1, fs1, fr1, g + 1)
        acc = chunk(3, chunk(2, acc))
        for j in range(2):
            for o in range(2):
                at = 128 * j + 64 * o
                bacc[2 * pairs[j] + o] = jnp.sum(acc[at : at + 64, :128].reshape(8, 8, 128), axis=0)
        row_transform(acc.astype(BF16), snd2, g)
        start_sibling(snd2, sib2, ss2, rs2, g)

    nt = (((1,), (1,)), ((), ()))

    def outer_block(block):
        at = pl.ds(block * 16, 16)
        return lax.dot_general(
            fbuf[:, at, :].reshape(256, 2048), gpbuf[:, at, :].reshape(256, 2048), nt,
            preferred_element_type=F32,
        )

    mix_bwd = spread_matrix(lw[...], False)

    def back_block(block):
        at = pl.ds(block * 16, 16)
        for w in range(0, 2048, STEP):
            part = dot(mix_bwd, gpbuf[:, at, w : w + STEP].reshape(256, STEP))
            fg_o[:, at, w : w + STEP] = part.astype(BF16).reshape(16, 16, STEP)

    lacc[...] = outer_block(0)
    pass_on(snd2, sib2, hb2, rcv2, rs2, ds2, dr2, GROUPS - 1)
    gradient_arrived(0)
    lacc[...] += outer_block(1)
    gradient_arrived(1)
    lacc[...] += outer_block(2)
    lacc[...] += outer_block(3)

    i = lax.broadcasted_iota(jnp.int32, (256, 256), 0)
    j = lax.broadcasted_iota(jnp.int32, (256, 256), 1)
    kept = jnp.where(i % 16 == j % 16, lacc[...], 0.0)
    kept = jnp.sum(kept.reshape(16, 16, 256), axis=1)
    i = lax.broadcasted_iota(jnp.int32, (256, 128), 0)
    j = lax.broadcasted_iota(jnp.int32, (256, 128), 1)
    pick = jnp.where(i // 16 == j, 1.0, 0.0).astype(F32)
    local = jnp.dot(kept, pick, preferred_element_type=F32, precision=lax.Precision.HIGHEST)
    first = jnp.sum(jnp.sum(bacc[...], axis=1)[:, :1], axis=1, keepdims=True)
    lane16 = lax.broadcasted_iota(jnp.int32, (16, 128), 1)
    pay[0] = jnp.where(lane16 == 16, first, local)
    to_sibling(pay.at[0], paysib, ps.at[0], pr.at[0])
    back_block(0)
    gradient_arrived(2)
    back_block(1)
    wait_for(paysib, pr.at[0])
    pay[1] = pay[0] + paysib[...]
    to_chips(lambda d: pay.at[1], payrow.at[chip], ps.at[1], pr.at[1])
    payrow[pl.ds(chip, 1)] = pay[pl.ds(1, 1)]
    back_block(2)
    back_block(3)

    gradient_arrived(GROUPS - 1)

    for g in range(GROUPS):
        for j in range(2):
            c = 4 * g + 2 * j
            parts = []
            for ref in (dfr, dfi):
                for k in range(2):
                    both = ref[c + k]
                    parts.append(both[:4] + both[4:])
            ga2[g, core, chip, 16 * j : 16 * j + 16, :] = jnp.concatenate(parts, axis=0).astype(BF16)
        gather_start(ga2, as2, ar2, g)

    wait_for(payrow.at[pl.ds(0, CHIPS - 1)], pr.at[1])
    pay[2] = jnp.sum(payrow[...], axis=0)
    for k in range(1, 8):
        pltpu.make_async_remote_copy(
            src_ref=pay.at[2], dst_ref=paydp.at[z], send_sem=ps.at[2], recv_sem=pr.at[2],
            device_id={"dp": lax.rem(z + k, 8)}, device_id_type=MESH,
        ).start()
    paydp[pl.ds(z, 1)] = pay[pl.ds(2, 1)]

    gather_forward(ga2, ar2, fs2, fr2, 0)
    for g in range(GROUPS):
        if g + 1 < GROUPS:
            gather_forward(ga2, ar2, fs2, fr2, g + 1)
        gather_end(ga2, fr2, g)
        ybuf[...] = row_inverse(ga2, g)
        for w in range(0, 2048, STEP):
            spectral = dot(ybuf[...], coli[:, w : w + STEP])
            local_part = fg_o[4 * g : 4 * g + 4, :, w : w + STEP].reshape(256, STEP).astype(F32)
            fg_o[4 * g : 4 * g + 4, :, w : w + STEP] = (
                (spectral + local_part).astype(BF16).reshape(4, 64, STEP)
            )

    wait_for(dwrcv.at[pl.ds(0, 7)], dwr)
    total = dwrcv[0].astype(F32)
    for k in range(1, 8):
        total = total + dwrcv[k].astype(F32)
    sg_o[...] = total.reshape(32, 8, 128)

    wait_for(paydp.at[pl.ds(0, 7)], pr.at[2])
    scale = 1.0 / math.sqrt(8 * 2048 * 2048)
    sums_o[...] = scale * jnp.sum(paydp[...], axis=0)

    for g in range(GROUPS):
        wait_for(snd1.at[g, 0], ss1.at[g])
        wait_for(hb1.at[g, pl.ds(0, CHIPS - 1)], ds1.at[g])
        wait_for(snd2.at[g, 0], ss2.at[g])
        wait_for(hb2.at[g, pl.ds(0, CHIPS - 1)], ds2.at[g])
        wait_for(ga1.at[g, core, pl.ds(0, CHIPS - 1)], as1.at[g])
        wait_for(ga1.at[g, core], fs1.at[g])
        wait_for(ga2.at[g, core, pl.ds(0, CHIPS - 1)], as2.at[g])
        wait_for(ga2.at[g, core], fs2.at[g])
    for slot in range(8):
        if OFFSETS[slot] != 0:
            wait_for(dwsnd.at[slot], dws.at[slot])
    wait_for(pay.at[0], ps.at[0])
    wait_for(payrow.at[pl.ds(0, CHIPS - 1)], ps.at[1])
    wait_for(paydp.at[pl.ds(0, 7)], ps.at[2])


def write_kernel(fg, sg, sums, fg_o, sg_o, lg_o, bg_o, sem):
    copy = pltpu.make_async_copy(fg, fg_o.at[0], sem)
    copy.start()
    sg_o[...] = sg[...]
    lg_o[...] = sums[:, :16]
    i = lax.broadcasted_iota(jnp.int32, (16, 16), 0)
    j = lax.broadcasted_iota(jnp.int32, (16, 16), 1)
    bg_o[...] = jnp.sum(jnp.where(i == j, sums[:, 16:17], 0.0), axis=0, keepdims=True)
    copy.wait()


def on_device(fields, cotangent, spectral, local_weight, bias):
    chans, rows, width = fields.shape[1:]
    modes = spectral.shape[4]
    height = rows * 2 * CHIPS
    scale = 1.0 / math.sqrt(height * width)
    colf, coli = column_tables(width, modes)
    rowf, rowi = row_tables(height, modes, 2 * CHIPS, scale)
    colf, coli, rowf, rowi = (jnp.asarray(t) for t in (colf, coli, rowf, rowi))
    anywhere = pl.BlockSpec(memory_space=pl.ANY)
    vmem = pl.BlockSpec(memory_space=pltpu.VMEM)
    dma = pltpu.SemaphoreType.DMA
    big = (16, 64, 2048)
    reduce_bufs = [
        pltpu.VMEM((GROUPS, 2, CHIPS, 32, 128), BF16),
        pltpu.VMEM((GROUPS, CHIPS, 32, 128), BF16),
        pltpu.VMEM((GROUPS, CHIPS, 32, 128), BF16),
        pltpu.VMEM((GROUPS, CHIPS, 32, 128), BF16),
    ]
    gather_buf = pltpu.VMEM((GROUPS, 2, CHIPS, 32, 128), BF16)
    tile16 = pltpu.VMEM((16, 8, 128), F32)
    scratch = [
        pltpu.VMEM((16, 16), BF16),
        pltpu.VMEM((1, 16), F32),
        pltpu.VMEM(big, BF16),
        pltpu.VMEM(big, BF16),
        pltpu.VMEM(big, F32),
        pltpu.VMEM(big, BF16),
        pltpu.VMEM((2, 1024, 128), BF16),
        pltpu.VMEM((2, 16, 8, 8, 128), F32),
        pltpu.VMEM(colf.shape, BF16),
        pltpu.VMEM(coli.shape, BF16),
        pltpu.VMEM(rowf.shape[1:], BF16),
        pltpu.VMEM(rowi.shape[1:], BF16),
        *reduce_bufs,
        *reduce_bufs,
        gather_buf,
        gather_buf,
        tile16,
        tile16,
        tile16,
        tile16,
        pltpu.VMEM((8, 16, 128), BF16),
        pltpu.VMEM((256, 256), BF16),
        tile16,
        pltpu.VMEM((256, 256), F32),
        pltpu.VMEM((8, 256, 128), BF16),
        pltpu.VMEM((8, 256, 128), BF16),
        pltpu.VMEM((3, 16, 128), F32),
        pltpu.VMEM((16, 128), F32),
        pltpu.VMEM((CHIPS, 16, 128), F32),
        pltpu.VMEM((8, 16, 128), F32),
        dma((GROUPS,)),
        dma((8,)),
        *[dma((GROUPS,)) for _ in range(16)],
        dma((8,)),
        dma(()),
        dma((3,)),
        dma((3,)),
    ]
    fg, sg, sums = pl.pallas_call(
        exchange_kernel,
        out_shape=(
            pltpu.VMEM(big, BF16),
            pltpu.VMEM((32, 8, 128), F32),
            pltpu.VMEM((16, 128), F32),
        ),
        in_specs=[anywhere] * 9,
        out_specs=(vmem, vmem, vmem),
        scratch_shapes=scratch,
        compiler_params=pltpu.CompilerParams(
            collective_id=0, has_side_effects=True, vmem_limit_bytes=117 * 2**19
        ),
        cost_estimate=pl.CostEstimate(flops=8 * 10**9, bytes_accessed=16 * 2**20, transcendentals=2**21),
        name="layer_exchange",
    )(
        fields[0], cotangent[0], spectral.reshape(2, 1024, 128), local_weight, bias[None, :],
        colf, coli, rowf, rowi,
    )
    grad, sg, lg, bg = pl.pallas_call(
        write_kernel,
        out_shape=(
            jax.ShapeDtypeStruct((1,) + big, BF16),
            jax.ShapeDtypeStruct((32, 8, 128), F32),
            jax.ShapeDtypeStruct((16, 16), F32),
            jax.ShapeDtypeStruct((1, 16), F32),
        ),
        in_specs=[anywhere, vmem, vmem],
        out_specs=(anywhere, vmem, vmem, vmem),
        scratch_shapes=[dma(())],
        compiler_params=pltpu.CompilerParams(vmem_limit_bytes=4 * 2**20),
        cost_estimate=pl.CostEstimate(flops=0, bytes_accessed=8 * 2**20, transcendentals=0),
        name="write_results",
    )(fg, sg, sums)
    return grad, sg.reshape(2, 16, 2, 4, 128), lg, bg.reshape(16)


def solution(mesh):
    finer = Mesh(mesh.devices.reshape(mesh.shape["dp"], 4, 4, 2), ("dp", "row_0", "row_1", "row_2"))
    placed = (
        P("dp", None, ROW, None),
        P("dp", None, ROW, None),
        P(None, None, None, ROW, None),
        P(),
        P(),
    )
    return jax.shard_map(
        on_device,
        mesh=finer,
        in_specs=placed,
        out_specs=(P("dp", None, ROW, None), P(None, None, "dp", ROW, None), P(), P()),
        check_vma=False,
    )
```

```python
import functools
import math

import jax
import jax.numpy as jnp
import ml_dtypes
import numpy as np
from jax import lax
from jax.experimental import pallas as pl
from jax.experimental.pallas import tpu as pltpu
from jax.sharding import Mesh
from jax.sharding import PartitionSpec as P

ROW = ("row_0", "row_1", "row_2")
MESH = pl.DeviceIdType.MESH
F32 = jnp.float32
BF16 = jnp.bfloat16
SIDE = 4
CHIPS = SIDE * SIDE
GROUPS = 4
OFFSETS = (4, 0, 3, 5, 2, 6, 1, 7)
STEP = 256
PEERS = sorted(
    ((dy, dx) for dy in range(SIDE) for dx in range(SIDE) if dy or dx),
    key=lambda p: -(min(p[0], SIDE - p[0]) + min(p[1], SIDE - p[1])),
)


def angles(freq, pos, count):
    turns = (freq[:, None] % count) * pos[None, :] % count
    return np.float32(2.0 * math.pi / count) * turns.astype(np.float32)


def column_tables(width, modes):
    angle = angles(np.arange(modes), np.arange(width), width)
    both = np.stack([np.cos(angle), -np.sin(angle)], axis=0).astype(ml_dtypes.bfloat16)
    inverse = both.reshape(2 * modes, width)
    return np.ascontiguousarray(inverse.T), inverse


def row_tables(height, modes, owners, scale):
    angle = angles(np.arange(modes) - modes // 2, np.arange(height), height)
    cos = np.cos(angle).astype(ml_dtypes.bfloat16).astype(np.float32) * scale
    sin = np.sin(angle).astype(ml_dtypes.bfloat16).astype(np.float32) * scale
    rows = height // owners
    each = modes // owners

    def split(table):
        table = table.reshape(CHIPS, 2, each, owners, rows)
        return table.transpose(3, 1, 0, 2, 4)

    cos, sin = split(cos), split(sin)
    forward = np.stack(
        [np.stack([cos, sin], axis=-2), np.stack([-sin, cos], axis=-2)], axis=3
    )
    half = forward.transpose(0, 5, 6, 1, 2, 3, 4)
    inverse = np.zeros((owners, 2) + half.shape[1:6] + (2, each), np.float32)
    for pair in range(2):
        inverse[:, pair, :, :, :, :, :, pair, :] = half
    forward = forward.reshape(owners, 2 * modes, 2 * rows)
    inverse = inverse.reshape(owners, 4 * rows, 4 * modes)
    return forward.astype(ml_dtypes.bfloat16), inverse.astype(ml_dtypes.bfloat16)


def dot(a, b):
    return jnp.dot(a, b, preferred_element_type=F32)


def wait_for(ref, sem):
    pltpu.make_async_copy(ref, ref, sem).wait()


def gelu_slope(x):
    k0 = math.sqrt(2.0 / math.pi)
    one = BF16
    x = x.astype(BF16)
    a = one(k0 * 0.044715) * (x * x)
    t = jnp.tanh(x * (a + one(k0)))
    q = x * (one(1.5) * a + one(0.5 * k0))
    return (one(1.0) + t) * (one(0.5) + q * (one(1.0) - t))


def spread_matrix(lw, transposed):
    i = lax.broadcasted_iota(jnp.int32, (256, 16), 0)
    j = lax.broadcasted_iota(jnp.int32, (256, 16), 1)
    pick = jnp.where(i // 16 == j, 1.0, 0.0).astype(BF16)
    if transposed:
        left = lax.dot_general(pick, lw, (((1,), (1,)), ((), ())), preferred_element_type=F32)
    else:
        left = dot(pick, lw)
    full = lax.dot_general(
        left.astype(BF16), pick, (((1,), (1,)), ((), ())), preferred_element_type=F32
    )
    i = lax.broadcasted_iota(jnp.int32, (256, 256), 0)
    j = lax.broadcasted_iota(jnp.int32, (256, 256), 1)
    return jnp.where(i % 16 == j % 16, full, 0.0).astype(BF16)


def exchange_kernel(
    fields, cot, spec, lw_h, bias_h, colf_h, coli_h, rowf_h, rowi_h,
    fg_o, sg_o, sums_o,
    lw, bias, fbuf, cbuf, lbuf, gpbuf, wbf, wf, colf, coli, rowf, rowi,
    snd1, sib1, hb1, rcv1, snd2, sib2, hb2, rcv2, ga1, ga2,
    frd, fid, dfr, dfi, gbuf, ybuf, bacc, lacc, dwsnd, dwrcv,
    pay, paysib, payrow, paydp,
    ld_f, ld,
    ss1, rs1, ss2, rs2, ds1, dr1, ds2, dr2,
    as1, ar1, fs1, fr1, as2, ar2, fs2, fr2, dws, dwr, ps, pr,
):
    z = lax.axis_index("dp")
    y = lax.axis_index("row_0")
    x = lax.axis_index("row_1")
    core = lax.axis_index("row_2")
    other = 1 - core
    chip = y * SIDE + x
    row = chip * 2 + core

    barrier = pltpu.get_barrier_semaphore()

    rows_y = [lax.rem(y + d, SIDE) for d in range(SIDE)]
    rows_x = [lax.rem(x + d, SIDE) for d in range(SIDE)]
    peers = [(rows_y[dy], rows_x[dx]) for dy, dx in PEERS]

    for ty, tx in peers:
        pl.semaphore_signal(
            barrier, inc=1, device_id={"row_0": ty, "row_1": tx}, device_id_type=MESH
        )
    pl.semaphore_signal(barrier, inc=1, device_id={"row_2": other}, device_id_type=MESH)
    for k in range(1, 8):
        pl.semaphore_signal(
            barrier, inc=1, device_id={"dp": lax.rem(z + k, 8)}, device_id_type=MESH
        )

    def load(src, dst, sem):
        copy = pltpu.make_async_copy(src, dst, sem)
        copy.start()
        return copy

    l_colf = load(colf_h, colf, ld.at[0])
    l_f = [load(fields.at[pl.ds(0, 4)], fbuf.at[pl.ds(0, 4)], ld_f.at[0])]
    l_rowf = load(rowf_h.at[row], rowf, ld.at[1])
    for g in range(1, GROUPS):
        l_f.append(load(fields.at[pl.ds(4 * g, 4)], fbuf.at[pl.ds(4 * g, 4)], ld_f.at[g]))
    l_w = load(spec, wbf, ld.at[2])
    l_lw = load(lw_h, lw, ld.at[6])
    l_bias = load(bias_h, bias, ld.at[7])
    l_rowi = load(rowi_h.at[row], rowi, ld.at[3])
    l_coli = load(coli_h, coli, ld.at[4])
    l_cot = load(cot, cbuf, ld.at[5])

    def to_sibling(src, dst, ssem, rsem):
        pltpu.make_async_remote_copy(
            src_ref=src, dst_ref=dst, send_sem=ssem, recv_sem=rsem,
            device_id={"row_2": other}, device_id_type=MESH,
        ).start()

    def to_chips(src_of, dst, ssem, rsem):
        for ty, tx in peers:
            pltpu.make_async_remote_copy(
                src_ref=src_of(ty * SIDE + tx), dst_ref=dst, send_sem=ssem, recv_sem=rsem,
                device_id={"row_0": ty, "row_1": tx}, device_id_type=MESH,
            ).start()

    def row_transform(xb, snd, g):
        for j in range(2):
            cols = []
            for c in range(2):
                at = 128 * j + 64 * c
                cols.append(jnp.concatenate([xb[at : at + 64, :128], xb[at : at + 64, 128:]], axis=0))
            p = dot(rowf[...], jnp.concatenate(cols, axis=1))
            blk = jnp.concatenate(
                [p[:, :128].reshape(32, 8, 128), p[:, 128:].reshape(32, 8, 128)], axis=1
            ).astype(BF16)
            snd[g, :, :, 16 * j : 16 * j + 16, :] = blk.reshape(2, CHIPS, 16, 128)

    def start_sibling(snd, sib, ss, rs, g):
        for half in range(2):
            at = pl.ds(half * (CHIPS // 2), CHIPS // 2)
            to_sibling(snd.at[g, other, at], sib.at[g, at], ss.at[g], rs.at[g])

    def pass_on(snd, sib, hb, rcv, rs, ds, dr, g):
        wait_for(sib.at[g], rs.at[g])
        hb[g] = (snd[g, core].astype(F32) + sib[g].astype(F32)).astype(BF16)
        to_chips(lambda d: hb.at[g, d], rcv.at[g, chip], ds.at[g], dr.at[g])
        rcv[g, pl.ds(chip, 1)] = hb[g, pl.ds(chip, 1)]

    def arrived(rcv, dr, g):
        wait_for(rcv.at[g, pl.ds(0, CHIPS - 1)], dr.at[g])
        return jnp.sum(rcv[g].astype(F32), axis=0)

    def gather_start(ga, asem, arsem, g):
        to_chips(lambda d: ga.at[g, core, chip], ga.at[g, core, chip], asem.at[g], arsem.at[g])

    def gather_forward(ga, arsem, fs, fr, g):
        wait_for(ga.at[g, core, pl.ds(0, CHIPS - 1)], arsem.at[g])
        for half in range(2):
            at = pl.ds(half * (CHIPS // 2), CHIPS // 2)
            to_sibling(ga.at[g, core, at], ga.at[g, core, at], fs.at[g], fr.at[g])

    def gather_end(ga, fr, g):
        wait_for(ga.at[g, other], fr.at[g])

    def row_inverse(ga, g):
        parts = [ga[g, :, :, 16 * j : 16 * j + 16, :].reshape(512, 128) for j in range(2)]
        out = dot(rowi[...], jnp.concatenate(parts, axis=1)).astype(BF16)
        rows = []
        for j in range(2):
            for o in range(2):
                block = out[128 * o : 128 * o + 128, 128 * j : 128 * j + 128]
                rows.append(jnp.concatenate([block[:64], block[64:]], axis=1))
        return jnp.concatenate(rows, axis=0)

    l_colf.wait()
    for g in range(GROUPS):
        l_f[g].wait()
        xb = dot(fbuf[4 * g : 4 * g + 4].reshape(256, 2048), colf[...]).astype(BF16)
        if g == 0:
            l_rowf.wait()
        row_transform(xb, snd1, g)
        if g == GROUPS - 2:
            pl.semaphore_wait(barrier, CHIPS + 7)
            for early in range(GROUPS - 1):
                start_sibling(snd1, sib1, ss1, rs1, early)
    start_sibling(snd1, sib1, ss1, rs1, GROUPS - 1)
    for g in range(GROUPS):
        pass_on(snd1, sib1, hb1, rcv1, rs1, ds1, dr1, g)

    l_lw.wait()
    l_bias.wait()
    i = lax.broadcasted_iota(jnp.int32, (256, 16), 0)
    j = lax.broadcasted_iota(jnp.int32, (256, 16), 1)
    bias_col = jnp.sum(jnp.where(i // 16 == j, bias[...], 0.0), axis=1, keepdims=True)
    mix_fwd = spread_matrix(lw[...], True)

    def local_block(block):
        at = pl.ds(pl.multiple_of(block * 16, 16), 16)
        for w in range(0, 2048, STEP):
            part = dot(mix_fwd, fbuf[:, at, w : w + STEP].reshape(256, STEP)) + bias_col
            lbuf[:, at, w : w + STEP] = part.reshape(16, 16, STEP)

    local_block(0)
    local_block(1)
    l_w.wait()

    def widen(c, carry):
        at = pl.ds(pl.multiple_of(c * 64, 64), 64)
        for part in range(2):
            wf[part, c] = wbf[part, at, :].astype(F32).reshape(8, 8, 128)
        return carry

    lax.fori_loop(0, 16, widen, 0)

    lane = lax.broadcasted_iota(jnp.int32, (8, 128), 1)
    double = jnp.where(lane == 0, 1.0, 2.0).astype(F32)

    def mix(c, carry):
        out_r, out_i = carry
        wr, wi = wf[0, c], wf[1, c]
        fr, fi = frd[c][None], fid[c][None]
        return out_r + wr * fr - wi * fi, out_i + wr * fi + wi * fr

    zero = jnp.zeros((8, 8, 128), F32)
    mixed = (zero, zero)
    for g in range(GROUPS):
        total = arrived(rcv1, dr1, g)
        for c in range(4):
            real = total[8 * c : 8 * c + 4]
            imag = total[8 * c + 4 : 8 * c + 8]
            frd[4 * g + c] = jnp.concatenate([real, real], axis=0)
            fid[4 * g + c] = jnp.concatenate([imag, imag], axis=0)
        mixed = lax.fori_loop(4 * g, 4 * g + 4, mix, mixed)
    mixed_r, mixed_i = mixed
    gbuf[...] = (jnp.concatenate([mixed_r, mixed_i], axis=1) * jnp.concatenate([double, double], axis=0)).astype(BF16)

    def pair_at(p):
        return lax.rem(z + OFFSETS[p], 8)

    for g in range(GROUPS):
        for j in range(2):
            ga1[g, core, chip, 16 * j : 16 * j + 16, :] = gbuf[pair_at(2 * g + j)]
        gather_start(ga1, as1, ar1, g)
    local_block(2)
    local_block(3)
    l_cot.wait()
    l_rowi.wait()
    l_coli.wait()
    gather_forward(ga1, ar1, fs1, fr1, 0)
    dfr[...] = jnp.zeros_like(dfr)
    dfi[...] = jnp.zeros_like(dfi)

    def input_terms(g):
        total = arrived(rcv2, dr2, g)
        modes = []
        for j in range(2):
            q = pair_at(2 * g + j)
            a, b = total[16 * j : 16 * j + 8], total[16 * j + 8 : 16 * j + 16]
            gr = jnp.concatenate([a[:4], b[:4]], axis=0) * double
            gi = jnp.concatenate([a[4:], b[4:]], axis=0) * double
            wr = wf[0, :, pl.ds(q, 1)].reshape(16, 8, 128)
            wi = wf[1, :, pl.ds(q, 1)].reshape(16, 8, 128)
            dfr[...] += wr * gr[None] + wi * gi[None]
            dfi[...] += wr * gi[None] - wi * gr[None]
            modes.append((gr, gi))
        return modes

    def weight_terms(g, modes):
        for j, (gr, gi) in enumerate(modes):
            slot = 2 * g + j
            fr, fi = frd[...], fid[...]
            term = jnp.concatenate(
                [
                    (gr[None] * fr + gi[None] * fi).reshape(128, 128),
                    (gi[None] * fr - gr[None] * fi).reshape(128, 128),
                ],
                axis=0,
            ).astype(BF16)
            if OFFSETS[slot] == 0:
                dwrcv[pl.ds(z, 1)] = term[None]
            else:
                dwsnd[slot] = term
                pltpu.make_async_remote_copy(
                    src_ref=dwsnd.at[slot], dst_ref=dwrcv.at[z], send_sem=dws.at[slot],
                    recv_sem=dwr, device_id={"dp": pair_at(slot)}, device_id_type=MESH,
                ).start()

    def gradient_arrived(g):
        weight_terms(g, input_terms(g))

    for g in range(GROUPS):
        gather_end(ga1, fr1, g)
        ybuf[...] = row_inverse(ga1, g)
        pairs = [pair_at(2 * g), pair_at(2 * g + 1)]

        def chunk(w, acc):
            at = pl.ds(w * STEP, STEP)
            out = dot(ybuf[...], coli[:, at])
            grads = []
            for j in range(2):
                o = pl.ds(2 * pairs[j], 2)
                pre = out[128 * j : 128 * j + 128] + lbuf[o, :, at].reshape(128, STEP)
                grad = cbuf[o, :, at].reshape(128, STEP) * gelu_slope(pre)
                gpbuf[o, :, at] = grad.reshape(2, 64, STEP)
                grads.append(grad)
            return acc + dot(jnp.concatenate(grads, axis=0), colf[at, :])

        if g + 1 < GROUPS:
            gather_forward(ga1, ar1, fs1, fr1, g + 1)
        acc = jnp.zeros((256, 256), F32)
        for w in range(2048 // STEP):
            if g > 0 and w == 6:
                pass_on(snd2, sib2, hb2, rcv2, rs2, ds2, dr2, g - 1)
            acc = chunk(w, acc)
        for j in range(2):
            for o in range(2):
                at = 128 * j + 64 * o
                bacc[2 * pairs[j] + o] = jnp.sum(acc[at : at + 64, :128].reshape(8, 8, 128), axis=0)
        row_transform(acc.astype(BF16), snd2, g)
        start_sibling(snd2, sib2, ss2, rs2, g)

    nt = (((1,), (1,)), ((), ()))

    def outer_block(block):
        at = pl.ds(block * 16, 16)
        return lax.dot_general(
            fbuf[:, at, :].reshape(256, 2048), gpbuf[:, at, :].reshape(256, 2048), nt,
            preferred_element_type=F32,
        )

    mix_bwd = spread_matrix(lw[...], False)

    def back_block(block):
        at = pl.ds(block * 16, 16)
        for w in range(0, 2048, STEP):
            part = dot(mix_bwd, gpbuf[:, at, w : w + STEP].reshape(256, STEP))
            fg_o[:, at, w : w + STEP] = part.astype(BF16).reshape(16, 16, STEP)

    lacc[...] = outer_block(0)
    gradient_arrived(0)
    pass_on(snd2, sib2, hb2, rcv2, rs2, ds2, dr2, GROUPS - 1)
    lacc[...] += outer_block(1)
    gradient_arrived(1)
    lacc[...] += outer_block(2)
    lacc[...] += outer_block(3)

    i = lax.broadcasted_iota(jnp.int32, (256, 256), 0)
    j = lax.broadcasted_iota(jnp.int32, (256, 256), 1)
    kept = jnp.where(i % 16 == j % 16, lacc[...], 0.0)
    kept = jnp.sum(kept.reshape(16, 16, 256), axis=1)
    i = lax.broadcasted_iota(jnp.int32, (256, 128), 0)
    j = lax.broadcasted_iota(jnp.int32, (256, 128), 1)
    pick = jnp.where(i // 16 == j, 1.0, 0.0).astype(F32)
    local = jnp.dot(kept, pick, preferred_element_type=F32, precision=lax.Precision.HIGHEST)
    first = jnp.sum(jnp.sum(bacc[...], axis=1)[:, :1], axis=1, keepdims=True)
    lane16 = lax.broadcasted_iota(jnp.int32, (16, 128), 1)
    pay[0] = jnp.where(lane16 == 16, first, local)
    to_sibling(pay.at[0], paysib, ps.at[0], pr.at[0])
    back_block(0)
    gradient_arrived(2)
    back_block(1)
    wait_for(paysib, pr.at[0])
    pay[1] = pay[0] + paysib[...]
    to_chips(lambda d: pay.at[1], payrow.at[chip], ps.at[1], pr.at[1])
    payrow[pl.ds(chip, 1)] = pay[pl.ds(1, 1)]
    back_block(2)
    back_block(3)

    last = input_terms(GROUPS - 1)

    for g in range(GROUPS):
        for j in range(2):
            c = 4 * g + 2 * j
            parts = []
            for ref in (dfr, dfi):
                for k in range(2):
                    both = ref[c + k]
                    parts.append(both[:4] + both[4:])
            ga2[g, core, chip, 16 * j : 16 * j + 16, :] = jnp.concatenate(parts, axis=0).astype(BF16)
        gather_start(ga2, as2, ar2, g)
    weight_terms(GROUPS - 1, last)

    wait_for(payrow.at[pl.ds(0, CHIPS - 1)], pr.at[1])
    pay[2] = jnp.sum(payrow[...], axis=0)
    for k in range(1, 8):
        pltpu.make_async_remote_copy(
            src_ref=pay.at[2], dst_ref=paydp.at[z], send_sem=ps.at[2], recv_sem=pr.at[2],
            device_id={"dp": lax.rem(z + k, 8)}, device_id_type=MESH,
        ).start()
    paydp[pl.ds(z, 1)] = pay[pl.ds(2, 1)]

    gather_forward(ga2, ar2, fs2, fr2, 0)
    for g in range(GROUPS):
        if g + 1 < GROUPS:
            gather_forward(ga2, ar2, fs2, fr2, g + 1)
        gather_end(ga2, fr2, g)
        ybuf[...] = row_inverse(ga2, g)
        for w in range(0, 2048, STEP):
            spectral = dot(ybuf[...], coli[:, w : w + STEP])
            local_part = fg_o[4 * g : 4 * g + 4, :, w : w + STEP].reshape(256, STEP).astype(F32)
            fg_o[4 * g : 4 * g + 4, :, w : w + STEP] = (
                (spectral + local_part).astype(BF16).reshape(4, 64, STEP)
            )

    wait_for(dwrcv.at[pl.ds(0, 7)], dwr)
    total = dwrcv[0].astype(F32)
    for k in range(1, 8):
        total = total + dwrcv[k].astype(F32)
    sg_o[...] = total.reshape(32, 8, 128)

    wait_for(paydp.at[pl.ds(0, 7)], pr.at[2])
    scale = 1.0 / math.sqrt(8 * 2048 * 2048)
    sums_o[...] = scale * jnp.sum(paydp[...], axis=0)

    for g in range(GROUPS):
        wait_for(snd1.at[g, 0], ss1.at[g])
        wait_for(hb1.at[g, pl.ds(0, CHIPS - 1)], ds1.at[g])
        wait_for(snd2.at[g, 0], ss2.at[g])
        wait_for(hb2.at[g, pl.ds(0, CHIPS - 1)], ds2.at[g])
        wait_for(ga1.at[g, core, pl.ds(0, CHIPS - 1)], as1.at[g])
        wait_for(ga1.at[g, core], fs1.at[g])
        wait_for(ga2.at[g, core, pl.ds(0, CHIPS - 1)], as2.at[g])
        wait_for(ga2.at[g, core], fs2.at[g])
    for slot in range(8):
        if OFFSETS[slot] != 0:
            wait_for(dwsnd.at[slot], dws.at[slot])
    wait_for(pay.at[0], ps.at[0])
    wait_for(payrow.at[pl.ds(0, CHIPS - 1)], ps.at[1])
    wait_for(paydp.at[pl.ds(0, 7)], ps.at[2])


def write_kernel(fg, sg, sums, fg_o, sg_o, lg_o, bg_o, sem):
    copy = pltpu.make_async_copy(fg, fg_o.at[0], sem)
    copy.start()
    sg_o[...] = sg[...]
    lg_o[...] = sums[:, :16]
    i = lax.broadcasted_iota(jnp.int32, (16, 16), 0)
    j = lax.broadcasted_iota(jnp.int32, (16, 16), 1)
    bg_o[...] = jnp.sum(jnp.where(i == j, sums[:, 16:17], 0.0), axis=0, keepdims=True)
    copy.wait()


def on_device(fields, cotangent, spectral, local_weight, bias):
    chans, rows, width = fields.shape[1:]
    modes = spectral.shape[4]
    height = rows * 2 * CHIPS
    scale = 1.0 / math.sqrt(height * width)
    colf, coli = column_tables(width, modes)
    rowf, rowi = row_tables(height, modes, 2 * CHIPS, scale)
    colf, coli, rowf, rowi = (jnp.asarray(t) for t in (colf, coli, rowf, rowi))
    anywhere = pl.BlockSpec(memory_space=pl.ANY)
    vmem = pl.BlockSpec(memory_space=pltpu.VMEM)
    dma = pltpu.SemaphoreType.DMA
    big = (16, 64, 2048)
    reduce_bufs = [
        pltpu.VMEM((GROUPS, 2, CHIPS, 32, 128), BF16),
        pltpu.VMEM((GROUPS, CHIPS, 32, 128), BF16),
        pltpu.VMEM((GROUPS, CHIPS, 32, 128), BF16),
        pltpu.VMEM((GROUPS, CHIPS, 32, 128), BF16),
    ]
    gather_buf = pltpu.VMEM((GROUPS, 2, CHIPS, 32, 128), BF16)
    tile16 = pltpu.VMEM((16, 8, 128), F32)
    scratch = [
        pltpu.VMEM((16, 16), BF16),
        pltpu.VMEM((1, 16), F32),
        pltpu.VMEM(big, BF16),
        pltpu.VMEM(big, BF16),
        pltpu.VMEM(big, F32),
        pltpu.VMEM(big, BF16),
        pltpu.VMEM((2, 1024, 128), BF16),
        pltpu.VMEM((2, 16, 8, 8, 128), F32),
        pltpu.VMEM(colf.shape, BF16),
        pltpu.VMEM(coli.shape, BF16),
        pltpu.VMEM(rowf.shape[1:], BF16),
        pltpu.VMEM(rowi.shape[1:], BF16),
        *reduce_bufs,
        *reduce_bufs,
        gather_buf,
        gather_buf,
        tile16,
        tile16,
        tile16,
        tile16,
        pltpu.VMEM((8, 16, 128), BF16),
        pltpu.VMEM((256, 256), BF16),
        tile16,
        pltpu.VMEM((256, 256), F32),
        pltpu.VMEM((8, 256, 128), BF16),
        pltpu.VMEM((8, 256, 128), BF16),
        pltpu.VMEM((3, 16, 128), F32),
        pltpu.VMEM((16, 128), F32),
        pltpu.VMEM((CHIPS, 16, 128), F32),
        pltpu.VMEM((8, 16, 128), F32),
        dma((GROUPS,)),
        dma((8,)),
        *[dma((GROUPS,)) for _ in range(16)],
        dma((8,)),
        dma(()),
        dma((3,)),
        dma((3,)),
    ]
    fg, sg, sums = pl.pallas_call(
        exchange_kernel,
        out_shape=(
            pltpu.VMEM(big, BF16),
            pltpu.VMEM((32, 8, 128), F32),
            pltpu.VMEM((16, 128), F32),
        ),
        in_specs=[anywhere] * 9,
        out_specs=(vmem, vmem, vmem),
        scratch_shapes=scratch,
        compiler_params=pltpu.CompilerParams(
            collective_id=0, has_side_effects=True, vmem_limit_bytes=117 * 2**19
        ),
        cost_estimate=pl.CostEstimate(flops=8 * 10**9, bytes_accessed=16 * 2**20, transcendentals=2**21),
        name="layer_exchange",
    )(
        fields[0], cotangent[0], spectral.reshape(2, 1024, 128), local_weight, bias[None, :],
        colf, coli, rowf, rowi,
    )
    grad, sg, lg, bg = pl.pallas_call(
        write_kernel,
        out_shape=(
            jax.ShapeDtypeStruct((1,) + big, BF16),
            jax.ShapeDtypeStruct((32, 8, 128), F32),
            jax.ShapeDtypeStruct((16, 16), F32),
            jax.ShapeDtypeStruct((1, 16), F32),
        ),
        in_specs=[anywhere, vmem, vmem],
        out_specs=(anywhere, vmem, vmem, vmem),
        scratch_shapes=[dma(())],
        compiler_params=pltpu.CompilerParams(vmem_limit_bytes=4 * 2**20),
        cost_estimate=pl.CostEstimate(flops=0, bytes_accessed=8 * 2**20, transcendentals=0),
        name="write_results",
    )(fg, sg, sums)
    return grad, sg.reshape(2, 16, 2, 4, 128), lg, bg.reshape(16)


def solution(mesh):
    finer = Mesh(mesh.devices.reshape(mesh.shape["dp"], 4, 4, 2), ("dp", "row_0", "row_1", "row_2"))
    placed = (
        P("dp", None, ROW, None),
        P("dp", None, ROW, None),
        P(None, None, None, ROW, None),
        P(),
        P(),
    )
    return jax.shard_map(
        on_device,
        mesh=finer,
        in_specs=placed,
        out_specs=(P("dp", None, ROW, None), P(None, None, "dp", ROW, None), P(), P()),
        check_vma=False,
    )
```

```python
import functools
import math

import jax
import jax.numpy as jnp
import ml_dtypes
import numpy as np
from jax import lax
from jax.experimental import pallas as pl
from jax.experimental.pallas import tpu as pltpu
from jax.sharding import Mesh
from jax.sharding import PartitionSpec as P

ROW = ("row_0", "row_1", "row_2")
MESH = pl.DeviceIdType.MESH
F32 = jnp.float32
BF16 = jnp.bfloat16
SIDE = 4
CHIPS = SIDE * SIDE
GROUPS = 4
OFFSETS = (4, 0, 3, 5, 2, 6, 1, 7)
STEP = 256
PEERS = sorted(
    ((dy, dx) for dy in range(SIDE) for dx in range(SIDE) if dy or dx),
    key=lambda p: -(min(p[0], SIDE - p[0]) + min(p[1], SIDE - p[1])),
)


def angles(freq, pos, count):
    turns = (freq[:, None] % count) * pos[None, :] % count
    return np.float32(2.0 * math.pi / count) * turns.astype(np.float32)


def column_tables(width, modes):
    angle = angles(np.arange(modes), np.arange(width), width)
    both = np.stack([np.cos(angle), -np.sin(angle)], axis=0).astype(ml_dtypes.bfloat16)
    inverse = both.reshape(2 * modes, width)
    return np.ascontiguousarray(inverse.T), inverse


def row_tables(height, modes, owners, scale):
    angle = angles(np.arange(modes) - modes // 2, np.arange(height), height)
    cos = np.cos(angle).astype(ml_dtypes.bfloat16).astype(np.float32) * scale
    sin = np.sin(angle).astype(ml_dtypes.bfloat16).astype(np.float32) * scale
    rows = height // owners
    each = modes // owners

    def split(table):
        table = table.reshape(CHIPS, 2, each, owners, rows)
        return table.transpose(3, 1, 0, 2, 4)

    cos, sin = split(cos), split(sin)
    forward = np.stack(
        [np.stack([cos, sin], axis=-2), np.stack([-sin, cos], axis=-2)], axis=3
    )
    half = forward.transpose(0, 5, 6, 1, 2, 3, 4)
    inverse = np.zeros((owners, 2) + half.shape[1:6] + (2, each), np.float32)
    for pair in range(2):
        inverse[:, pair, :, :, :, :, :, pair, :] = half
    forward = forward.reshape(owners, 2 * modes, 2 * rows)
    inverse = inverse.reshape(owners, 4 * rows, 4 * modes)
    return forward.astype(ml_dtypes.bfloat16), inverse.astype(ml_dtypes.bfloat16)


def dot(a, b):
    return jnp.dot(a, b, preferred_element_type=F32)


def wait_for(ref, sem):
    pltpu.make_async_copy(ref, ref, sem).wait()


def gelu_slope(x):
    k0 = math.sqrt(2.0 / math.pi)
    one = BF16
    x = x.astype(BF16)
    a = one(k0 * 0.044715) * (x * x)
    t = jnp.tanh(x * (a + one(k0)))
    q = x * (one(1.5) * a + one(0.5 * k0))
    return (one(1.0) + t) * (one(0.5) + q * (one(1.0) - t))


def spread_matrix(lw, transposed):
    i = lax.broadcasted_iota(jnp.int32, (256, 16), 0)
    j = lax.broadcasted_iota(jnp.int32, (256, 16), 1)
    pick = jnp.where(i // 16 == j, 1.0, 0.0).astype(BF16)
    if transposed:
        left = lax.dot_general(pick, lw, (((1,), (1,)), ((), ())), preferred_element_type=F32)
    else:
        left = dot(pick, lw)
    full = lax.dot_general(
        left.astype(BF16), pick, (((1,), (1,)), ((), ())), preferred_element_type=F32
    )
    i = lax.broadcasted_iota(jnp.int32, (256, 256), 0)
    j = lax.broadcasted_iota(jnp.int32, (256, 256), 1)
    return jnp.where(i % 16 == j % 16, full, 0.0).astype(BF16)


def exchange_kernel(
    fields, cot, spec, lw_h, bias_h, colf_h, coli_h, rowf_h, rowi_h,
    fg_o, sg_o, sums_o,
    lw, bias, fbuf, cbuf, lbuf, gpbuf, wbf, wf, colf, coli, rowf, rowi,
    snd1, sib1, hb1, rcv1, snd2, sib2, hb2, rcv2, ga1, ga2,
    frd, fid, dfr, dfi, gbuf, ybuf, bacc, lacc, dwsnd, dwrcv,
    pay, paysib, payrow, paydp,
    ld_f, ld,
    ss1, rs1, ss2, rs2, ds1, dr1, ds2, dr2,
    as1, ar1, fs1, fr1, as2, ar2, fs2, fr2, dws, dwr, ps, pr,
):
    z = lax.axis_index("dp")
    y = lax.axis_index("row_0")
    x = lax.axis_index("row_1")
    core = lax.axis_index("row_2")
    other = 1 - core
    chip = y * SIDE + x
    row = chip * 2 + core

    barrier = pltpu.get_barrier_semaphore()

    rows_y = [lax.rem(y + d, SIDE) for d in range(SIDE)]
    rows_x = [lax.rem(x + d, SIDE) for d in range(SIDE)]
    peers = [(rows_y[dy], rows_x[dx]) for dy, dx in PEERS]

    for ty, tx in peers:
        pl.semaphore_signal(
            barrier, inc=1, device_id={"row_0": ty, "row_1": tx}, device_id_type=MESH
        )
    pl.semaphore_signal(barrier, inc=1, device_id={"row_2": other}, device_id_type=MESH)
    for k in range(1, 8):
        pl.semaphore_signal(
            barrier, inc=1, device_id={"dp": lax.rem(z + k, 8)}, device_id_type=MESH
        )

    def load(src, dst, sem):
        copy = pltpu.make_async_copy(src, dst, sem)
        copy.start()
        return copy

    l_colf = load(colf_h, colf, ld.at[0])
    l_f = [load(fields.at[pl.ds(0, 4)], fbuf.at[pl.ds(0, 4)], ld_f.at[0])]
    l_rowf = load(rowf_h.at[row], rowf, ld.at[1])
    for g in range(1, GROUPS):
        l_f.append(load(fields.at[pl.ds(4 * g, 4)], fbuf.at[pl.ds(4 * g, 4)], ld_f.at[g]))
    l_w = load(spec, wbf, ld.at[2])
    l_lw = load(lw_h, lw, ld.at[6])
    l_bias = load(bias_h, bias, ld.at[7])
    l_rowi = load(rowi_h.at[row], rowi, ld.at[3])
    l_coli = load(coli_h, coli, ld.at[4])
    l_cot = load(cot, cbuf, ld.at[5])

    def to_sibling(src, dst, ssem, rsem):
        pltpu.make_async_remote_copy(
            src_ref=src, dst_ref=dst, send_sem=ssem, recv_sem=rsem,
            device_id={"row_2": other}, device_id_type=MESH,
        ).start()

    def to_chips(src_of, dst, ssem, rsem):
        for ty, tx in peers:
            pltpu.make_async_remote_copy(
                src_ref=src_of(ty * SIDE + tx), dst_ref=dst, send_sem=ssem, recv_sem=rsem,
                device_id={"row_0": ty, "row_1": tx}, device_id_type=MESH,
            ).start()

    def row_transform(xb, snd, g):
        for j in range(2):
            cols = []
            for c in range(2):
                at = 128 * j + 64 * c
                cols.append(jnp.concatenate([xb[at : at + 64, :128], xb[at : at + 64, 128:]], axis=0))
            p = dot(rowf[...], jnp.concatenate(cols, axis=1))
            blk = jnp.concatenate(
                [p[:, :128].reshape(32, 8, 128), p[:, 128:].reshape(32, 8, 128)], axis=1
            ).astype(BF16)
            snd[g, :, :, 16 * j : 16 * j + 16, :] = blk.reshape(2, CHIPS, 16, 128)

    def start_sibling(snd, sib, ss, rs, g):
        for half in range(2):
            at = pl.ds(half * (CHIPS // 2), CHIPS // 2)
            to_sibling(snd.at[g, other, at], sib.at[g, at], ss.at[g], rs.at[g])

    def pass_on(snd, sib, hb, rcv, rs, ds, dr, g):
        wait_for(sib.at[g], rs.at[g])
        hb[g] = (snd[g, core].astype(F32) + sib[g].astype(F32)).astype(BF16)
        to_chips(lambda d: hb.at[g, d], rcv.at[g, chip], ds.at[g], dr.at[g])
        rcv[g, pl.ds(chip, 1)] = hb[g, pl.ds(chip, 1)]

    def arrived(rcv, dr, g):
        wait_for(rcv.at[g, pl.ds(0, CHIPS - 1)], dr.at[g])
        return jnp.sum(rcv[g].astype(F32), axis=0)

    def gather_start(ga, asem, arsem, g):
        to_chips(lambda d: ga.at[g, core, chip], ga.at[g, core, chip], asem.at[g], arsem.at[g])

    def gather_forward(ga, arsem, fs, fr, g):
        wait_for(ga.at[g, core, pl.ds(0, CHIPS - 1)], arsem.at[g])
        for half in range(2):
            at = pl.ds(half * (CHIPS // 2), CHIPS // 2)
            to_sibling(ga.at[g, core, at], ga.at[g, core, at], fs.at[g], fr.at[g])

    def gather_end(ga, fr, g):
        wait_for(ga.at[g, other], fr.at[g])

    def row_inverse(ga, g):
        parts = [ga[g, :, :, 16 * j : 16 * j + 16, :].reshape(512, 128) for j in range(2)]
        out = dot(rowi[...], jnp.concatenate(parts, axis=1)).astype(BF16)
        rows = []
        for j in range(2):
            for o in range(2):
                block = out[128 * o : 128 * o + 128, 128 * j : 128 * j + 128]
                rows.append(jnp.concatenate([block[:64], block[64:]], axis=1))
        return jnp.concatenate(rows, axis=0)

    l_colf.wait()
    for g in range(GROUPS):
        l_f[g].wait()
        xb = dot(fbuf[4 * g : 4 * g + 4].reshape(256, 2048), colf[...]).astype(BF16)
        if g == 0:
            l_rowf.wait()
        row_transform(xb, snd1, g)
        if g == GROUPS - 2:
            pl.semaphore_wait(barrier, CHIPS + 7)
            for early in range(GROUPS - 1):
                start_sibling(snd1, sib1, ss1, rs1, early)
    start_sibling(snd1, sib1, ss1, rs1, GROUPS - 1)
    for g in range(GROUPS):
        pass_on(snd1, sib1, hb1, rcv1, rs1, ds1, dr1, g)

    l_lw.wait()
    l_bias.wait()
    i = lax.broadcasted_iota(jnp.int32, (256, 16), 0)
    j = lax.broadcasted_iota(jnp.int32, (256, 16), 1)
    bias_col = jnp.sum(jnp.where(i // 16 == j, bias[...], 0.0), axis=1, keepdims=True)
    mix_fwd = spread_matrix(lw[...], True)

    def local_block(block):
        at = pl.ds(pl.multiple_of(block * 16, 16), 16)
        for w in range(0, 2048, STEP):
            part = dot(mix_fwd, fbuf[:, at, w : w + STEP].reshape(256, STEP)) + bias_col
            lbuf[:, at, w : w + STEP] = part.reshape(16, 16, STEP)

    local_block(0)
    local_block(1)
    l_w.wait()

    def widen(c, carry):
        at = pl.ds(pl.multiple_of(c * 64, 64), 64)
        for part in range(2):
            wf[part, c] = wbf[part, at, :].astype(F32).reshape(8, 8, 128)
        return carry

    lax.fori_loop(0, 16, widen, 0)

    lane = lax.broadcasted_iota(jnp.int32, (8, 128), 1)
    double = jnp.where(lane == 0, 1.0, 2.0).astype(F32)

    def mix(c, carry):
        out_r, out_i = carry
        wr, wi = wf[0, c], wf[1, c]
        fr, fi = frd[c][None], fid[c][None]
        return out_r + wr * fr - wi * fi, out_i + wr * fi + wi * fr

    zero = jnp.zeros((8, 8, 128), F32)
    mixed = (zero, zero)
    for g in range(GROUPS):
        total = arrived(rcv1, dr1, g)
        for c in range(4):
            real = total[8 * c : 8 * c + 4]
            imag = total[8 * c + 4 : 8 * c + 8]
            frd[4 * g + c] = jnp.concatenate([real, real], axis=0)
            fid[4 * g + c] = jnp.concatenate([imag, imag], axis=0)
        mixed = lax.fori_loop(4 * g, 4 * g + 4, mix, mixed)
    mixed_r, mixed_i = mixed
    gbuf[...] = (jnp.concatenate([mixed_r, mixed_i], axis=1) * jnp.concatenate([double, double], axis=0)).astype(BF16)

    def pair_at(p):
        return lax.rem(z + OFFSETS[p], 8)

    for g in range(GROUPS):
        for j in range(2):
            ga1[g, core, chip, 16 * j : 16 * j + 16, :] = gbuf[pair_at(2 * g + j)]
        gather_start(ga1, as1, ar1, g)
    local_block(2)
    local_block(3)
    l_cot.wait()
    l_rowi.wait()
    l_coli.wait()
    gather_forward(ga1, ar1, fs1, fr1, 0)
    dfr[...] = jnp.zeros_like(dfr)
    dfi[...] = jnp.zeros_like(dfi)

    def input_terms(g):
        total = arrived(rcv2, dr2, g)
        modes = []
        for j in range(2):
            q = pair_at(2 * g + j)
            a, b = total[16 * j : 16 * j + 8], total[16 * j + 8 : 16 * j + 16]
            gr = jnp.concatenate([a[:4], b[:4]], axis=0) * double
            gi = jnp.concatenate([a[4:], b[4:]], axis=0) * double
            wr = wf[0, :, pl.ds(q, 1)].reshape(16, 8, 128)
            wi = wf[1, :, pl.ds(q, 1)].reshape(16, 8, 128)
            dfr[...] += wr * gr[None] + wi * gi[None]
            dfi[...] += wr * gi[None] - wi * gr[None]
            modes.append((gr, gi))
        return modes

    def weight_terms(g, modes):
        for j, (gr, gi) in enumerate(modes):
            slot = 2 * g + j
            fr, fi = frd[...], fid[...]
            term = jnp.concatenate(
                [
                    (gr[None] * fr + gi[None] * fi).reshape(128, 128),
                    (gi[None] * fr - gr[None] * fi).reshape(128, 128),
                ],
                axis=0,
            ).astype(BF16)
            if OFFSETS[slot] == 0:
                dwrcv[pl.ds(z, 1)] = term[None]
            else:
                dwsnd[slot] = term
                pltpu.make_async_remote_copy(
                    src_ref=dwsnd.at[slot], dst_ref=dwrcv.at[z], send_sem=dws.at[slot],
                    recv_sem=dwr, device_id={"dp": pair_at(slot)}, device_id_type=MESH,
                ).start()

    def gradient_arrived(g):
        weight_terms(g, input_terms(g))

    for g in range(GROUPS):
        gather_end(ga1, fr1, g)
        ybuf[...] = row_inverse(ga1, g)
        pairs = [pair_at(2 * g), pair_at(2 * g + 1)]

        def chunk(w, acc):
            at = pl.ds(w * STEP, STEP)
            out = dot(ybuf[...], coli[:, at])
            grads = []
            for j in range(2):
                o = pl.ds(2 * pairs[j], 2)
                pre = out[128 * j : 128 * j + 128] + lbuf[o, :, at].reshape(128, STEP)
                grad = cbuf[o, :, at].reshape(128, STEP) * gelu_slope(pre)
                gpbuf[o, :, at] = grad.reshape(2, 64, STEP)
                grads.append(grad)
            return acc + dot(jnp.concatenate(grads, axis=0), colf[at, :])

        if g + 1 < GROUPS:
            gather_forward(ga1, ar1, fs1, fr1, g + 1)
        acc = jnp.zeros((256, 256), F32)
        for w in range(2048 // STEP):
            if g > 0 and w == 6:
                pass_on(snd2, sib2, hb2, rcv2, rs2, ds2, dr2, g - 1)
            acc = chunk(w, acc)
        for j in range(2):
            for o in range(2):
                at = 128 * j + 64 * o
                bacc[2 * pairs[j] + o] = jnp.sum(acc[at : at + 64, :128].reshape(8, 8, 128), axis=0)
        row_transform(acc.astype(BF16), snd2, g)
        start_sibling(snd2, sib2, ss2, rs2, g)

    nt = (((1,), (1,)), ((), ()))

    def outer_block(block):
        at = pl.ds(block * 16, 16)
        return lax.dot_general(
            fbuf[:, at, :].reshape(256, 2048), gpbuf[:, at, :].reshape(256, 2048), nt,
            preferred_element_type=F32,
        )

    mix_bwd = spread_matrix(lw[...], False)

    def back_block(block):
        at = pl.ds(block * 16, 16)
        for w in range(0, 2048, STEP):
            part = dot(mix_bwd, gpbuf[:, at, w : w + STEP].reshape(256, STEP))
            fg_o[:, at, w : w + STEP] = part.astype(BF16).reshape(16, 16, STEP)

    lacc[...] = outer_block(0)
    gradient_arrived(0)
    pass_on(snd2, sib2, hb2, rcv2, rs2, ds2, dr2, GROUPS - 1)
    lacc[...] += outer_block(1)
    gradient_arrived(1)
    lacc[...] += outer_block(2)
    lacc[...] += outer_block(3)

    i = lax.broadcasted_iota(jnp.int32, (256, 256), 0)
    j = lax.broadcasted_iota(jnp.int32, (256, 256), 1)
    kept = jnp.where(i % 16 == j % 16, lacc[...], 0.0)
    kept = jnp.sum(kept.reshape(16, 16, 256), axis=1)
    i = lax.broadcasted_iota(jnp.int32, (256, 128), 0)
    j = lax.broadcasted_iota(jnp.int32, (256, 128), 1)
    pick = jnp.where(i // 16 == j, 1.0, 0.0).astype(F32)
    local = jnp.dot(kept, pick, preferred_element_type=F32, precision=lax.Precision.HIGHEST)
    first = jnp.sum(jnp.sum(bacc[...], axis=1)[:, :1], axis=1, keepdims=True)
    lane16 = lax.broadcasted_iota(jnp.int32, (16, 128), 1)
    pay[0] = jnp.where(lane16 == 16, first, local)
    to_sibling(pay.at[0], paysib, ps.at[0], pr.at[0])
    back_block(0)
    gradient_arrived(2)
    back_block(1)
    wait_for(paysib, pr.at[0])
    pay[1] = pay[0] + paysib[...]
    to_chips(lambda d: pay.at[1], payrow.at[chip], ps.at[1], pr.at[1])
    payrow[pl.ds(chip, 1)] = pay[pl.ds(1, 1)]
    back_block(2)
    back_block(3)

    last = input_terms(GROUPS - 1)

    for g in range(GROUPS):
        for j in range(2):
            c = 4 * g + 2 * j
            parts = []
            for ref in (dfr, dfi):
                for k in range(2):
                    both = ref[c + k]
                    parts.append(both[:4] + both[4:])
            ga2[g, core, chip, 16 * j : 16 * j + 16, :] = jnp.concatenate(parts, axis=0).astype(BF16)
        gather_start(ga2, as2, ar2, g)
    weight_terms(GROUPS - 1, last)

    wait_for(payrow.at[pl.ds(0, CHIPS - 1)], pr.at[1])
    pay[2] = jnp.sum(payrow[...], axis=0)
    for k in range(1, 8):
        pltpu.make_async_remote_copy(
            src_ref=pay.at[2], dst_ref=paydp.at[z], send_sem=ps.at[2], recv_sem=pr.at[2],
            device_id={"dp": lax.rem(z + k, 8)}, device_id_type=MESH,
        ).start()
    paydp[pl.ds(z, 1)] = pay[pl.ds(2, 1)]

    gather_forward(ga2, ar2, fs2, fr2, 0)
    for g in range(GROUPS):
        if g + 1 < GROUPS:
            gather_forward(ga2, ar2, fs2, fr2, g + 1)
        if g == GROUPS - 1:
            wait_for(dwrcv.at[pl.ds(0, 7)], dwr)
            total = dwrcv[0].astype(F32)
            for k in range(1, 8):
                total = total + dwrcv[k].astype(F32)
            sg_o[...] = total.reshape(32, 8, 128)
            for k in range(GROUPS):
                wait_for(snd1.at[k, 0], ss1.at[k])
                wait_for(hb1.at[k, pl.ds(0, CHIPS - 1)], ds1.at[k])
                wait_for(snd2.at[k, 0], ss2.at[k])
                wait_for(hb2.at[k, pl.ds(0, CHIPS - 1)], ds2.at[k])
                wait_for(ga1.at[k, core, pl.ds(0, CHIPS - 1)], as1.at[k])
                wait_for(ga1.at[k, core], fs1.at[k])
            for slot in range(8):
                if OFFSETS[slot] != 0:
                    wait_for(dwsnd.at[slot], dws.at[slot])
        gather_end(ga2, fr2, g)
        ybuf[...] = row_inverse(ga2, g)
        for w in range(0, 2048, STEP):
            spectral = dot(ybuf[...], coli[:, w : w + STEP])
            local_part = fg_o[4 * g : 4 * g + 4, :, w : w + STEP].reshape(256, STEP).astype(F32)
            fg_o[4 * g : 4 * g + 4, :, w : w + STEP] = (
                (spectral + local_part).astype(BF16).reshape(4, 64, STEP)
            )

    wait_for(paydp.at[pl.ds(0, 7)], pr.at[2])
    scale = 1.0 / math.sqrt(8 * 2048 * 2048)
    sums_o[...] = scale * jnp.sum(paydp[...], axis=0)

    for g in range(GROUPS):
        wait_for(ga2.at[g, core, pl.ds(0, CHIPS - 1)], as2.at[g])
        wait_for(ga2.at[g, core], fs2.at[g])
    wait_for(pay.at[0], ps.at[0])
    wait_for(payrow.at[pl.ds(0, CHIPS - 1)], ps.at[1])
    wait_for(paydp.at[pl.ds(0, 7)], ps.at[2])


def write_kernel(fg, sg, sums, fg_o, sg_o, lg_o, bg_o, sem):
    copy = pltpu.make_async_copy(fg, fg_o.at[0], sem)
    copy.start()
    sg_o[...] = sg[...]
    lg_o[...] = sums[:, :16]
    i = lax.broadcasted_iota(jnp.int32, (16, 16), 0)
    j = lax.broadcasted_iota(jnp.int32, (16, 16), 1)
    bg_o[...] = jnp.sum(jnp.where(i == j, sums[:, 16:17], 0.0), axis=0, keepdims=True)
    copy.wait()


def on_device(fields, cotangent, spectral, local_weight, bias):
    chans, rows, width = fields.shape[1:]
    modes = spectral.shape[4]
    height = rows * 2 * CHIPS
    scale = 1.0 / math.sqrt(height * width)
    colf, coli = column_tables(width, modes)
    rowf, rowi = row_tables(height, modes, 2 * CHIPS, scale)
    colf, coli, rowf, rowi = (jnp.asarray(t) for t in (colf, coli, rowf, rowi))
    anywhere = pl.BlockSpec(memory_space=pl.ANY)
    vmem = pl.BlockSpec(memory_space=pltpu.VMEM)
    dma = pltpu.SemaphoreType.DMA
    big = (16, 64, 2048)
    reduce_bufs = [
        pltpu.VMEM((GROUPS, 2, CHIPS, 32, 128), BF16),
        pltpu.VMEM((GROUPS, CHIPS, 32, 128), BF16),
        pltpu.VMEM((GROUPS, CHIPS, 32, 128), BF16),
        pltpu.VMEM((GROUPS, CHIPS, 32, 128), BF16),
    ]
    gather_buf = pltpu.VMEM((GROUPS, 2, CHIPS, 32, 128), BF16)
    tile16 = pltpu.VMEM((16, 8, 128), F32)
    scratch = [
        pltpu.VMEM((16, 16), BF16),
        pltpu.VMEM((1, 16), F32),
        pltpu.VMEM(big, BF16),
        pltpu.VMEM(big, BF16),
        pltpu.VMEM(big, F32),
        pltpu.VMEM(big, BF16),
        pltpu.VMEM((2, 1024, 128), BF16),
        pltpu.VMEM((2, 16, 8, 8, 128), F32),
        pltpu.VMEM(colf.shape, BF16),
        pltpu.VMEM(coli.shape, BF16),
        pltpu.VMEM(rowf.shape[1:], BF16),
        pltpu.VMEM(rowi.shape[1:], BF16),
        *reduce_bufs,
        *reduce_bufs,
        gather_buf,
        gather_buf,
        tile16,
        tile16,
        tile16,
        tile16,
        pltpu.VMEM((8, 16, 128), BF16),
        pltpu.VMEM((256, 256), BF16),
        tile16,
        pltpu.VMEM((256, 256), F32),
        pltpu.VMEM((8, 256, 128), BF16),
        pltpu.VMEM((8, 256, 128), BF16),
        pltpu.VMEM((3, 16, 128), F32),
        pltpu.VMEM((16, 128), F32),
        pltpu.VMEM((CHIPS, 16, 128), F32),
        pltpu.VMEM((8, 16, 128), F32),
        dma((GROUPS,)),
        dma((8,)),
        *[dma((GROUPS,)) for _ in range(16)],
        dma((8,)),
        dma(()),
        dma((3,)),
        dma((3,)),
    ]
    fg, sg, sums = pl.pallas_call(
        exchange_kernel,
        out_shape=(
            pltpu.VMEM(big, BF16),
            pltpu.VMEM((32, 8, 128), F32),
            pltpu.VMEM((16, 128), F32),
        ),
        in_specs=[anywhere] * 9,
        out_specs=(vmem, vmem, vmem),
        scratch_shapes=scratch,
        compiler_params=pltpu.CompilerParams(
            collective_id=0, has_side_effects=True, vmem_limit_bytes=117 * 2**19
        ),
        cost_estimate=pl.CostEstimate(flops=8 * 10**9, bytes_accessed=16 * 2**20, transcendentals=2**21),
        name="layer_exchange",
    )(
        fields[0], cotangent[0], spectral.reshape(2, 1024, 128), local_weight, bias[None, :],
        colf, coli, rowf, rowi,
    )
    grad, sg, lg, bg = pl.pallas_call(
        write_kernel,
        out_shape=(
            jax.ShapeDtypeStruct((1,) + big, BF16),
            jax.ShapeDtypeStruct((32, 8, 128), F32),
            jax.ShapeDtypeStruct((16, 16), F32),
            jax.ShapeDtypeStruct((1, 16), F32),
        ),
        in_specs=[anywhere, vmem, vmem],
        out_specs=(anywhere, vmem, vmem, vmem),
        scratch_shapes=[dma(())],
        compiler_params=pltpu.CompilerParams(vmem_limit_bytes=4 * 2**20),
        cost_estimate=pl.CostEstimate(flops=0, bytes_accessed=8 * 2**20, transcendentals=0),
        name="write_results",
    )(fg, sg, sums)
    return grad, sg.reshape(2, 16, 2, 4, 128), lg, bg.reshape(16)


def solution(mesh):
    finer = Mesh(mesh.devices.reshape(mesh.shape["dp"], 4, 4, 2), ("dp", "row_0", "row_1", "row_2"))
    placed = (
        P("dp", None, ROW, None),
        P("dp", None, ROW, None),
        P(None, None, None, ROW, None),
        P(),
        P(),
    )
    return jax.shard_map(
        on_device,
        mesh=finer,
        in_specs=placed,
        out_specs=(P("dp", None, ROW, None), P(None, None, "dp", ROW, None), P(), P()),
        check_vma=False,
    )
```
